512 devices in a mesh: sample: 16 (over x, y_lo, core), space: 32 (over y_hi, z).
Axes of the slice: x: 4, y: 4 (y_hi: 2, y_lo: 2; y = y_hi * 2 + y_lo), z: 16, core: 2. Of those that a mesh axis runs over, the one named last changes fastest.
Arguments:
- fields: bfloat16 [16, 4, 64, 24, 256], P('sample', None, 'space'), may hold values from -6 to 6
- cotangent: bfloat16 [16, 4, 64, 24, 256], P('sample', None, 'space'), may hold values from -6 to 6
- w_in: bfloat16 [27, 32, 4], replicated, may hold values from -0.625 to 0.625
- w_down: bfloat16 [8, 64, 32], replicated, may hold values from -0.375 to 0.375
- w_coarse: bfloat16 [27, 64, 64], replicated, may hold values from -0.15625 to 0.15625
- w_up: bfloat16 [8, 32, 64], replicated, may hold values from -0.75 to 0.75
- w_out: bfloat16 [4, 32], replicated, may hold values from -1 to 1
Outputs:
- prediction: bfloat16 [16, 4, 64, 24, 256], P('sample', None, 'space')
- grad_in: float32 [27, 32, 4], replicated
- grad_down: float32 [8, 64, 32], replicated
- grad_coarse: float32 [27, 64, 64], replicated
- grad_up: float32 [8, 32, 64], replicated
- grad_out: float32 [4, 32], replicated
The draws below stay inside these ranges and needn't reach their ends.
All inputs are finite; a program needn't handle non-finite values.
Results may differ from the reference program's by a relative error of at most 0.018.
Values may be sent and summed in bfloat16 or wider, within the bound.
A program may use at most 64 MiB of HBM per device.

```python
import jax
import jax.numpy as jnp
from jax import lax

FIELDS = 4
C1 = 32
C2 = 64
NY = 24
NZ = 256
NX = 64
BATCH = 16


def levels(rng, extent, cuts, low, largest):
    factor_of, own = 1.0, jax.random.fold_in(rng, 6)
    for axis_at, blocks in cuts:
        heights = jnp.exp(jax.random.uniform(jax.random.fold_in(own, axis_at), (blocks,), jnp.float32, low / len(cuts), largest / len(cuts)))
        factor_of = factor_of * jnp.repeat(heights, extent[axis_at] // blocks).reshape([-1 if axis == axis_at else 1 for axis in range(len(extent))])
    return factor_of


def bell_draw(own_key, extent, scale, limit, cuts=(), kind=jnp.bfloat16):
    drawn = jax.random.normal(own_key, extent, jnp.float32) * scale
    if len(cuts) > 0:
        drawn = levels(own_key, extent, cuts, -0.22, 0.18) * drawn
    return jnp.clip(drawn, min=-limit, max=limit).astype(kind)


def setup_inputs(seed: int = 0) -> dict:
    streams_of = jax.random.split(jax.random.key(seed), 8)
    return {
        "fields": bell_draw(streams_of[0], (BATCH, FIELDS, NX, NY, NZ), 1.0, 6.0, ((0, 16), (2, 32))),
        "cotangent": bell_draw(streams_of[1], (BATCH, FIELDS, NX, NY, NZ), 1.0, 6.0, ((0, 16), (2, 32))),
        "w_in": bell_draw(streams_of[2], (27, C1, FIELDS), (27 * FIELDS) ** -0.5, 0.625),
        "w_down": bell_draw(streams_of[3], (8, C2, C1), (8 * C1) ** -0.5, 0.375),
        "w_coarse": bell_draw(streams_of[4], (27, C2, C2), (27 * C2) ** -0.5, 0.15625),
        "w_up": bell_draw(streams_of[5], (8, C1, C2), C2 ** -0.5, 0.75),
        "w_out": bell_draw(streams_of[6], (FIELDS, C1), C1 ** -0.5, 1.0),
    }


def pad_cube(volume):
    return jnp.pad(volume, ((0, 0), (1, 1), (1, 1), (1, 1)))

def offsets(number):
    return (number // 9, number // 3 % 3, number % 3)

def conv_cube(padded, weights, dims):
    depth, height, width = dims
    summed = jnp.zeros((weights.shape[1], depth, height, width), jnp.float32)
    for number in range(27):
        first, second, third = offsets(number)
        window = padded[:, first:first + depth, second:second + height, third:third + width].astype(jnp.float32)
        summed = summed + jnp.einsum('oc,cxyz->oxyz', weights[number].astype(jnp.float32), window, precision=lax.Precision.HIGHEST)
    return summed

def conv_weight_grad(gradient, padded, dims):
    depth, height, width = dims
    pieces = []
    for number in range(27):
        first, second, third = offsets(number)
        window = padded[:, first:first + depth, second:second + height, third:third + width].astype(jnp.float32)
        pieces.append(jnp.einsum('oxyz,cxyz->oc', gradient.astype(jnp.float32), window, precision=lax.Precision.HIGHEST))
    return jnp.stack(pieces)

def conv_data_grad(grad_padded, weights, dims):
    depth, height, width = dims
    summed = jnp.zeros((weights.shape[2], depth, height, width), jnp.float32)
    for number in range(27):
        first, second, third = offsets(number)
        window = grad_padded[:, 2 - first:2 - first + depth, 2 - second:2 - second + height, 2 - third:2 - third + width].astype(jnp.float32)
        summed = summed + jnp.einsum('oc,oxyz->cxyz', weights[number].astype(jnp.float32), window, precision=lax.Precision.HIGHEST)
    return summed

def silu_slope(value):
    sigma = jax.nn.sigmoid(value)
    return sigma * (1.0 + value * (1.0 - sigma))

def one_sample(volume, cot_volume, weights):
    w_in, w_down, w_coarse, w_up, w_out = weights
    chan_fine = w_in.shape[1]
    chan_coarse = w_coarse.shape[1]
    depth, height, width = (volume.shape[1], volume.shape[2], volume.shape[3])
    fine_dims = (depth, height, width)
    coarse_dims = (depth // 2, height // 2, width // 2)
    hp = lax.Precision.HIGHEST
    down_five = w_down.reshape(2, 2, 2, chan_coarse, chan_fine).astype(jnp.float32)
    up_five = w_up.reshape(2, 2, 2, chan_fine, chan_coarse).astype(jnp.float32)
    field_pad = pad_cube(volume)
    pre_fine = conv_cube(field_pad, w_in, fine_dims)
    act_fine = jax.nn.silu(pre_fine).astype(jnp.bfloat16)
    act_six = act_fine.reshape(chan_fine, coarse_dims[0], 2, coarse_dims[1], 2, coarse_dims[2], 2).astype(jnp.float32)
    reduced = jnp.einsum('ijkoc,cxiyjzk->oxyz', down_five, act_six, precision=hp).astype(jnp.bfloat16)
    reduced_pad = pad_cube(reduced)
    pre_coarse = conv_cube(reduced_pad, w_coarse, coarse_dims)
    act_coarse = jax.nn.silu(pre_coarse).astype(jnp.bfloat16)
    upward = jnp.einsum('ijkoc,cxyz->oxiyjzk', up_five, act_coarse.astype(jnp.float32), precision=hp).reshape(chan_fine, depth, height, width)
    merged = (act_fine.astype(jnp.float32) + upward).astype(jnp.bfloat16)
    w_out_f = w_out.astype(jnp.float32)
    cot_f = cot_volume.astype(jnp.float32)
    prediction = jnp.einsum('fc,cxyz->fxyz', w_out_f, merged.astype(jnp.float32), precision=hp).astype(jnp.bfloat16)
    grad_out = jnp.einsum('fxyz,cxyz->fc', cot_f, merged.astype(jnp.float32), precision=hp)
    back_merged = jnp.einsum('fc,fxyz->cxyz', w_out_f, cot_f, precision=hp).astype(jnp.bfloat16)
    back_six = back_merged.reshape(chan_fine, coarse_dims[0], 2, coarse_dims[1], 2, coarse_dims[2], 2).astype(jnp.float32)
    grad_up = jnp.einsum('oxiyjzk,cxyz->ijkoc', back_six, act_coarse.astype(jnp.float32), precision=hp).reshape(8, chan_fine, chan_coarse)
    coarse_term = jnp.einsum('ijkoc,oxiyjzk->cxyz', up_five, back_six, precision=hp)
    back_coarse = (coarse_term * silu_slope(pre_coarse)).astype(jnp.bfloat16)
    grad_coarse = conv_weight_grad(back_coarse, reduced_pad, coarse_dims)
    back_reduced = conv_data_grad(pad_cube(back_coarse), w_coarse, coarse_dims).astype(jnp.bfloat16)
    grad_down = jnp.einsum('oxyz,cxiyjzk->ijkoc', back_reduced.astype(jnp.float32), act_six, precision=hp).reshape(8, chan_coarse, chan_fine)
    spread = jnp.einsum('ijkoc,oxyz->cxiyjzk', down_five, back_reduced.astype(jnp.float32), precision=hp).reshape(chan_fine, depth, height, width)
    back_fine = ((back_merged.astype(jnp.float32) + spread) * silu_slope(pre_fine)).astype(jnp.bfloat16)
    grad_in = conv_weight_grad(back_fine, field_pad, fine_dims)
    return (prediction, (grad_in, grad_down, grad_coarse, grad_up, grad_out))

def reference(fields, cotangent, w_in, w_down, w_coarse, w_up, w_out):
    weights = (w_in, w_down, w_coarse, w_up, w_out)

    def advance(running, sample_pair):
        prediction, gradients = one_sample(sample_pair[0], sample_pair[1], weights)
        return (tuple((left + right for left, right in zip(running, gradients))), prediction)
    start_sums = tuple((jnp.zeros(weight.shape, jnp.float32) for weight in weights))
    totals, predictions = lax.scan(advance, start_sums, (fields, cotangent))
    return (predictions, totals[0], totals[1], totals[2], totals[3], totals[4])
```

```python
import functools

import jax
import jax.numpy as jnp
import numpy as np
from jax import lax
from jax.experimental import pallas as pl
from jax.experimental.pallas import tpu as pltpu
from jax.sharding import PartitionSpec as P

MESH = pl.DeviceIdType.MESH
BF = jnp.bfloat16
F32 = jnp.float32
LANES = 128
CHUNK = 256
HIGH = 2


def dot(a, b):
    return lax.dot_general(a, b, (((1,), (0,)), ((), ())), preferred_element_type=F32)


def dot_nt(a, b):
    return lax.dot_general(a, b, (((1,), (1,)), ((), ())), preferred_element_type=F32)


def one_hots(ny, nz, nf):
    wide = nz // 2
    rows = (ny + 2) * 4 * nf
    perm = np.zeros((rows, 4 * nf * ny), np.float32)
    own = 2 * nf * ny
    for y in range(ny):
        for f in range(nf):
            for dx in range(4):
                if dx == 0:
                    source = own + f * ny + y
                elif dx == 3:
                    source = own + nf * ny + f * ny + y
                else:
                    source = (f * 2 + dx - 1) * ny + y
                perm[(y + 1) * 4 * nf + dx * nf + f, source] = 1
    perm2 = np.zeros((2 * nf * ny, 2 * nf * ny), np.float32)
    for y in range(ny):
        for x in range(2):
            for f in range(nf):
                perm2[y * 2 * nf + x * nf + f, (f * 2 + x) * ny + y] = 1
    split = np.zeros((nz, 4 * wide), np.float32)
    for d in range(4):
        for z in range(wide):
            if 0 <= 2 * z + d - 1 < nz:
                split[2 * z + d - 1, d * wide + z] = 1
    join = split[:, wide : 3 * wide].T.copy()
    fold = np.zeros((128, 8 * 64 * nf), np.float32)
    for m in range(8):
        mz, my, mx = m // 4, m // 2 % 2, m % 2
        for k in range(27):
            dx, dy, dz = k // 9 + mx, k // 3 % 3 + my, k % 3 + mz
            for c in range(nf):
                fold[k * nf + c, m * 64 * nf + (dy * 4 + dz) * 4 * nf + dx * nf + c] = 1
    return [jnp.asarray(v, BF) for v in (perm, perm2, perm2.T.copy(), split, join, fold)]


def part_of(m):
    return 4 * (m % 2) + 2 * (m // 2 % 2) + m // 4


def body(
    ns, nspace,
    fields, cot, w_in, w_dn, w_co, w_up, w_out, perm, perm2, perm2t, split, join, fold,
    pred, g_in, g_dn, g_co, g_up, g_out,
    f_land, ff, tt, patches, win, win_t, wdt, wd, wu, wut, bd, bdt, wf, wb, wa,
    act, slope, cots, cot_t, bm, term, red, r_land, bc, b_land, rolled, act_c, pred_t, bf,
    red_out, bc_out,
    gi_wide, gc, e_send, e_recv, l_send, l_recv, late, z_send, z_recv, z_out, z_all,
    e_out, e_all, l_out, l_all, full,
    halo_ss, halo_rs, e_ss, e_rs, l_ss, l_rs, z_ss, z_rs, y_ss, y_rs, a_ss, a_rs, b_ss, b_rs,
):
    nzg = nspace // HIGH
    nxy = ns * HIGH
    s = lax.axis_index("sample")
    sp = lax.axis_index("space")
    high, zi = sp // nzg, lax.rem(sp, nzg)
    me = high * ns + s
    left = lax.rem(sp + nspace - 1, nspace)
    right = lax.rem(sp + 1, nspace)
    has_left = jnp.where(sp > 0, 1.0, 0.0).astype(F32)
    has_right = jnp.where(sp < nspace - 1, 1.0, 0.0).astype(F32)

    def plane_peer(i):
        peer = lax.rem(me + i, nxy)
        return peer, (lax.rem(peer, ns), (peer // ns) * nzg + zi)

    def z_peer(i):
        peer = lax.rem(zi + i, nzg)
        return peer, (s, high * nzg + peer)

    barrier = pltpu.get_barrier_semaphore()

    def greet(device):
        pl.semaphore_signal(barrier, inc=1, device_id=device, device_id_type=MESH)

    greet((s, left))
    greet((s, right))

    def greet_plane(i, carry):
        greet(plane_peer(i)[1])
        return carry

    def greet_z(i, carry):
        greet(z_peer(i)[1])
        return carry

    lax.fori_loop(1, nxy, greet_plane, 0)
    lax.fori_loop(1, nzg, greet_z, 0)
    pl.semaphore_wait(barrier, 2 + nxy - 1 + nzg - 1)

    def halo(step, to_left, to_right, land):
        copies = [
            pltpu.make_async_remote_copy(
                src_ref=to_right, dst_ref=land.at[0], send_sem=halo_ss.at[2 * step],
                recv_sem=halo_rs.at[2 * step], device_id=(s, right), device_id_type=MESH,
            ),
            pltpu.make_async_remote_copy(
                src_ref=to_left, dst_ref=land.at[1], send_sem=halo_ss.at[2 * step + 1],
                recv_sem=halo_rs.at[2 * step + 1], device_id=(s, left), device_id_type=MESH,
            ),
        ]
        for copy in copies:
            copy.start()
        return copies

    def finish(copies):
        for copy in copies:
            copy.wait()

    nf, ny, nz = fields.shape[1], fields.shape[3], fields.shape[4]
    c1, c2 = w_up.shape[1], w_up.shape[2]
    yc = ny // 2
    cells = yc * LANES
    chunks = cells // CHUNK
    fr = 4 * nf
    hr = 2 * nf

    f_copies = halo(0, fields.at[0, :, 0], fields.at[0, :, 1], f_land)

    win_t[...] = jnp.zeros_like(win_t)
    for k in range(27):
        win_t[k * nf : (k + 1) * nf, 0:c1] = w_in[k].astype(F32)
    flat = win_t[...].T[0:c1, :].astype(BF)
    spread_w = dot(flat, fold[...]).astype(BF)
    for m in range(8):
        win[m * c1 : (m + 1) * c1, :] = spread_w[:, m * 64 * nf : (m + 1) * 64 * nf]
        wdt[m * c1 : (m + 1) * c1, :] = w_dn[part_of(m)]
        wu[m * c1 : (m + 1) * c1, :] = w_up[part_of(m)]
    wd[...] = wdt[...].astype(F32).T.astype(BF)
    wut[...] = wu[...].astype(F32).T.astype(BF)
    bd[...] = jnp.zeros_like(bd)
    for m in range(8):
        bd[m * nf : (m + 1) * nf, m * c1 : (m + 1) * c1] = w_out[...].astype(F32)
    bdt[...] = bd[...].T.astype(BF)
    bd_b = bd[...].astype(BF)
    for q in range(3):
        for a in range(3):
            wf[q, :, a * c2 : (a + 1) * c2] = jnp.concatenate(
                [w_co[9 * a + 3 * q + b] for b in range(3)], axis=0
            ).astype(F32)
            for b in range(3):
                wa[q, a * c2 : (a + 1) * c2, b * c2 : (b + 1) * c2] = w_co[
                    9 * (2 - a) + 3 * (2 - q) + b
                ].astype(F32)
        wb[q] = wa[q].T.astype(BF)

    cot_rows = cot[0].astype(F32).reshape(2 * nf * ny, nz).astype(BF)
    cot_t[...] = dot(dot(perm2[...], cot_rows).astype(BF), split[:, LANES : 3 * LANES]).astype(BF)
    for y in range(yc):
        for m in range(2):
            cots[m * 2 * hr : (m + 1) * 2 * hr, y * LANES : (y + 1) * LANES] = cot_t[
                y * 2 * hr : (y + 1) * 2 * hr, m * LANES : (m + 1) * LANES
            ]
    for n in range(chunks):
        at = slice(n * CHUNK, (n + 1) * CHUNK)
        back = dot(bdt[...], cots[:, at]).astype(BF)
        bm[:, at] = back
        term[:, at] = dot(wut[...], back)

    rows = nf * ny
    ff[0 : 2 * rows, :] = fields[0].astype(F32).reshape(2 * rows, nz).astype(BF)
    finish(f_copies)
    ff[2 * rows : 3 * rows, :] = (f_land[0].astype(F32).reshape(rows, nz) * has_left).astype(BF)
    ff[3 * rows : 4 * rows, :] = (f_land[1].astype(F32).reshape(rows, nz) * has_right).astype(BF)
    tt[...] = dot(dot(perm[...], ff[...]).astype(BF), split[...]).astype(BF)
    for y in range(yc):
        for dy in range(4):
            for dz in range(4):
                patches[(dy * 4 + dz) * fr : (dy * 4 + dz + 1) * fr, y * LANES : (y + 1) * LANES] = tt[
                    (2 * y + dy) * fr : (2 * y + dy + 1) * fr, dz * LANES : (dz + 1) * LANES
                ]
    for n in range(chunks):
        at = slice(n * CHUNK, (n + 1) * CHUNK)
        pre = dot(win[...], patches[:, at])
        sigma = jax.nn.sigmoid(pre)
        fine = (pre * sigma).astype(BF)
        slope[:, at] = sigma * (1.0 + pre * (1.0 - sigma))
        act[:, at] = fine
        red_out[:, at] = dot(wd[...], fine).astype(BF)
    r_copies = halo(1, red_out, red_out, r_land)
    edge = jnp.zeros((3 * c2, LANES), BF)
    for planes in (red, bc):
        planes[:, 0:LANES] = edge
        planes[:, LANES + cells : 2 * LANES + cells] = edge
    inner = slice(LANES, LANES + cells)
    red[c2 : 2 * c2, inner] = red_out[...]
    finish(r_copies)
    red[0:c2, inner] = (r_land[0].astype(F32) * has_left).astype(BF)
    red[2 * c2 : 3 * c2, inner] = (r_land[1].astype(F32) * has_right).astype(BF)

    lane = lax.rem(lax.broadcasted_iota(jnp.int32, (c2, CHUNK), 1), LANES)
    not_first, not_last = lane > 0, lane < LANES - 1

    def later(v):
        return jnp.where(not_first, pltpu.roll(v, 1, 1), 0.0)

    def sooner(v):
        return jnp.where(not_last, pltpu.roll(v, CHUNK - 1, 1), 0.0)

    wf_b = [wf[q].astype(BF) for q in range(3)]

    for n in range(chunks):
        at = slice(n * CHUNK, (n + 1) * CHUNK)
        out = sum(
            dot(wf_b[q], red[:, n * CHUNK + q * LANES : (n + 1) * CHUNK + q * LANES])
            for q in range(3)
        )
        pre = out[c2 : 2 * c2] + later(out[0:c2]) + sooner(out[2 * c2 : 3 * c2])
        sigma = jax.nn.sigmoid(pre)
        act_c[:, at] = (pre * sigma).astype(BF)
        back = (term[:, at] * (sigma * (1.0 + pre * (1.0 - sigma)))).astype(BF)
        bc_out[:, at] = back
        wide = back.astype(F32)
        rolled[0:c2, at] = sooner(wide).astype(BF)
        rolled[c2 : 2 * c2, at] = back
        rolled[2 * c2 : 3 * c2, at] = later(wide).astype(BF)
    b_copies = halo(2, bc_out, bc_out, b_land)
    bc[c2 : 2 * c2, inner] = bc_out[...]

    for q in range(3):
        gc[q * 3 * c2 : (q + 1) * 3 * c2, :] = dot_nt(
            rolled[...], red[:, q * LANES : q * LANES + cells]
        )
    g_out_wide = jnp.zeros((8 * nf, 8 * c1), F32)
    for n in range(chunks):
        at = slice(n * CHUNK, (n + 1) * CHUNK)
        merged = (act[:, at].astype(F32) + dot(wu[...], act_c[:, at])).astype(BF)
        out = dot(bd_b, merged).astype(BF)
        g_out_wide = g_out_wide + dot_nt(cots[:, at], merged)
        for y in range(CHUNK // LANES):
            for m in range(2):
                pred_t[
                    (n * (CHUNK // LANES) + y) * 2 * hr : (n * (CHUNK // LANES) + y + 1) * 2 * hr,
                    m * LANES : (m + 1) * LANES,
                ] = out[m * 2 * hr : (m + 1) * 2 * hr, y * LANES : (y + 1) * LANES]
    gu = dot_nt(bm[...], act_c[...])
    mine = (
        lax.broadcasted_iota(jnp.int32, (8 * nf, 8 * c1), 0) // nf
        == lax.broadcasted_iota(jnp.int32, (8 * nf, 8 * c1), 1) // c1
    )
    g_out_wide = jnp.where(mine, g_out_wide, 0.0)
    g_out_half = g_out_wide[:, 0:LANES] + g_out_wide[:, LANES : 2 * LANES]
    g_out_half = g_out_half + pltpu.roll(g_out_half, 64, 1)
    g_out_half = g_out_half + pltpu.roll(g_out_half, 32, 1)
    g_out_half = g_out_half[0:8] + g_out_half[8:16] + g_out_half[16:24] + g_out_half[24:32]
    g_out_half = g_out_half + pltpu.roll(g_out_half, 4, 0)

    e_rows = e_send.shape[1]
    full[0 : 9 * c2, :] = gc[:, 0:LANES]
    half = 9 * c2 // 2
    full[9 * c2 : 9 * c2 + half, 0:c2] = gc[0:half, LANES : LANES + c2]
    full[9 * c2 : 9 * c2 + half, c2 : 2 * c2] = gc[half : 2 * half, LANES : LANES + c2]
    up_at = 9 * c2 + half
    full[up_at : up_at + LANES, 0:c2] = gu[0:LANES]
    full[up_at : up_at + LANES, c2 : 2 * c2] = gu[LANES : 2 * LANES]
    out_at = up_at + LANES
    full[out_at : out_at + 8, :] = g_out_half
    full[out_at + 8 : out_at + 32, :] = jnp.zeros((24, LANES), F32)
    e_send[...] = full[...].reshape(nxy, e_rows, LANES).astype(BF)

    def plane_copy(i, src, dst, send_sem, recv_sem):
        return pltpu.make_async_remote_copy(
            src_ref=src, dst_ref=dst, send_sem=send_sem, recv_sem=recv_sem,
            device_id=plane_peer(i)[1], device_id_type=MESH,
        )

    def send_early(i, carry):
        plane_copy(i, e_send.at[plane_peer(i)[0]], e_recv.at[i], e_ss, e_rs).start()
        return carry

    lax.fori_loop(1, nxy, send_early, 0)
    e_recv[0] = e_send[me]

    finish(b_copies)
    bc[0:c2, inner] = (b_land[0].astype(F32) * has_left).astype(BF)
    bc[2 * c2 : 3 * c2, inner] = (b_land[1].astype(F32) * has_right).astype(BF)
    for n in range(chunks):
        at = slice(n * CHUNK, (n + 1) * CHUNK)
        out = sum(
            dot(wb[q], bc[:, n * CHUNK + q * LANES : (n + 1) * CHUNK + q * LANES])
            for q in range(3)
        )
        back = out[c2 : 2 * c2] + sooner(out[0:c2]) + later(out[2 * c2 : 3 * c2])
        back = back.astype(BF)
        bc_out_at = rolled
        bc_out_at[0:c2, at] = back
        bf[:, at] = ((bm[:, at].astype(F32) + dot(wdt[...], back)) * slope[:, at]).astype(BF)
    gd = dot_nt(act[...], rolled[0:c2, :])
    late[0:LANES, 0:c2] = gd[0:LANES]
    late[0:LANES, c2 : 2 * c2] = gd[LANES : 2 * LANES]
    gi = dot_nt(bf[...], patches[...]).astype(BF)
    for m in range(8):
        gi_wide[:, m * 64 * nf : (m + 1) * 64 * nf] = gi[m * c1 : (m + 1) * c1, :]
    late[LANES : LANES + c1, :] = dot_nt(gi_wide[...], fold[...])
    l_rows = (LANES + c1) // nxy
    for p in range(nxy):
        l_send[p, 0:l_rows, :] = late[p * l_rows : (p + 1) * l_rows, :]

    def send_late(i, carry):
        plane_copy(i, l_send.at[plane_peer(i)[0]], l_recv.at[i], l_ss, l_rs).start()
        return carry

    lax.fori_loop(1, nxy, send_late, 0)
    l_recv[0] = l_send[me]

    out = dot(dot(perm2t[...], pred_t[...]).astype(BF), join[...])
    pred[0] = out.reshape(nf, 2, ny, nz).astype(BF)

    def all_of(ref, sem, count):
        block = ref.at[pl.ds(0, count)]
        pltpu.make_async_copy(block, block, sem).wait()

    all_of(e_recv, e_rs, nxy - 1)
    early_sum = jnp.sum(e_recv[...].astype(F32), axis=0)
    all_of(l_recv, l_rs, nxy - 1)
    late_sum = jnp.sum(l_recv[...], axis=0)

    z_rows = -(-(e_rows + l_rows) // nzg)
    full[0:e_rows, :] = early_sum
    full[e_rows : e_rows + l_rows, :] = late_sum[0:l_rows]
    for j in range(nzg):
        z_send[j, 0:z_rows, :] = full[j * z_rows : (j + 1) * z_rows, :]

    def send_z(i, carry):
        peer, device = z_peer(i)
        pltpu.make_async_remote_copy(
            src_ref=z_send.at[peer], dst_ref=z_recv.at[i], send_sem=z_ss, recv_sem=z_rs,
            device_id=device, device_id_type=MESH,
        ).start()
        return carry

    lax.fori_loop(1, nzg, send_z, 0)
    z_recv[0] = z_send[zi]
    all_of(z_recv, z_rs, nzg - 1)
    total = jnp.sum(z_recv[...], axis=0)
    z_out[...] = total
    z_all[zi] = total

    def spread_z(i, carry):
        pltpu.make_async_remote_copy(
            src_ref=z_out, dst_ref=z_all.at[zi], send_sem=y_ss, recv_sem=y_rs,
            device_id=z_peer(i)[1], device_id_type=MESH,
        ).start()
        return carry

    lax.fori_loop(1, nzg, spread_z, 0)
    all_of(z_all, y_rs, nzg - 1)
    for j in range(nzg):
        full[j * z_rows : (j + 1) * z_rows, :] = z_all[j, 0:z_rows, :]
    e_out[...] = full[0:e_rows, :].astype(BF)
    l_out[0:l_rows, :] = full[e_rows : e_rows + l_rows, :]
    e_all[me] = e_out[...]
    l_all[me] = l_out[...]

    def spread_plane(i, carry):
        plane_copy(i, e_out, e_all.at[me], a_ss, a_rs).start()
        plane_copy(i, l_out, l_all.at[me], b_ss, b_rs).start()
        return carry

    lax.fori_loop(1, nxy, spread_plane, 0)

    all_of(e_send, e_ss, nxy - 1)
    all_of(l_send, l_ss, nxy - 1)
    all_of(z_send, z_ss, nzg - 1)
    all_of(z_all, y_ss, nzg - 1)
    all_of(e_all, a_rs, nxy - 1)
    all_of(l_all, b_rs, nxy - 1)
    all_of(e_all, a_ss, nxy - 1)
    all_of(l_all, b_ss, nxy - 1)

    full[...] = e_all[...].astype(F32).reshape(nxy * e_rows, LANES)
    for q in range(3):
        for b in range(3):
            row = (q * 3 + b) * c2
            block = full[row : row + c2, :]
            g_co[3 * q + b] = block[:, 0:c2]
            g_co[9 + 3 * q + b] = pltpu.roll(block, c2, 1)[:, 0:c2]
    for n in range(9):
        row = 9 * c2 + (n * c2) % half
        lo = min(c2, half - (n * c2) % half)
        first, side = n * c2 // half, None
        block = full[row : row + lo, :]
        if first == 1:
            block = pltpu.roll(block, c2, 1)
        g_co[18 + n, 0:lo, :] = block[:, 0:c2]
        if lo < c2:
            rest = pltpu.roll(full[9 * c2 : 9 * c2 + c2 - lo, :], c2, 1)
            g_co[18 + n, lo:c2, :] = rest[:, 0:c2]
    for m in range(4):
        block = full[up_at + m * c1 : up_at + (m + 1) * c1, :]
        g_up[part_of(m)] = block[:, 0:c2]
        g_up[part_of(m + 4)] = pltpu.roll(block, c2, 1)[:, 0:c2]
    g_out[...] = full[out_at : out_at + nf, 0:c1]
    for p in range(nxy):
        late[p * l_rows : (p + 1) * l_rows, :] = l_all[p, 0:l_rows, :]
    for m in range(4):
        block = late[m * c1 : (m + 1) * c1, :]
        g_dn[part_of(m)] = block[:, 0:c2]
        g_dn[part_of(m + 4)] = pltpu.roll(block, c2, 1)[:, 0:c2]
    win_t[0:c1, :] = late[LANES : LANES + c1, :]
    flipped = win_t[...].T
    for k in range(27):
        g_in[k] = flipped[k * nf : (k + 1) * nf, 0:c1]


def shards(fields, cotangent, w_in, w_down, w_coarse, w_up, w_out):
    ns, nspace = lax.axis_size("sample"), lax.axis_size("space")
    nf, ny, nz = fields.shape[1], fields.shape[3], fields.shape[4]
    c1, c2 = w_up.shape[1], w_up.shape[2]
    cells = (ny // 2) * (nz // 2)
    nxy, nzg = ns * HIGH, nspace // HIGH
    e_rows = (9 * c2 * 3 // 2 + LANES + 32) // nxy
    l_rows = (LANES + c1) // nxy
    z_rows = -(-(e_rows + l_rows) // nzg)
    zr = -(-z_rows // 4) * 4 if z_rows > 4 else 4
    if zr > 4:
        zr = -(-zr // 8) * 8
    lr = -(-l_rows // 8) * 8
    wide = 64 * nf
    consts = one_hots(ny, nz, nf)
    vm = pltpu.VMEM
    dma = pltpu.SemaphoreType.DMA
    scratch = [
        vm((2, nf, ny, nz), BF),
        vm((4 * nf * ny, nz), BF),
        vm(((ny + 2) * 4 * nf, 4 * LANES), BF),
        vm((wide, cells), BF),
        vm((8 * c1, wide), BF),
        vm((128, 128), F32),
        vm((8 * c1, c2), BF),
        vm((c2, 8 * c1), BF),
        vm((8 * c1, c2), BF),
        vm((c2, 8 * c1), BF),
        vm((8 * nf, 8 * c1), F32),
        vm((8 * c1, 8 * nf), BF),
        vm((3, 3 * c2, 3 * c2), F32),
        vm((3, 3 * c2, 3 * c2), BF),
        vm((3, 3 * c2, 3 * c2), F32),
        vm((8 * c1, cells), BF),
        vm((8 * c1, cells), F32),
        vm((8 * nf, cells), BF),
        vm((2 * nf * ny, 2 * LANES), BF),
        vm((8 * c1, cells), BF),
        vm((c2, cells), F32),
        vm((3 * c2, cells + 2 * LANES), BF),
        vm((2, c2, cells), BF),
        vm((3 * c2, cells + 2 * LANES), BF),
        vm((2, c2, cells), BF),
        vm((3 * c2, cells), BF),
        vm((c2, cells), BF),
        vm((2 * nf * ny, 2 * LANES), BF),
        vm((8 * c1, cells), BF),
        vm((c2, cells), BF),
        vm((c2, cells), BF),
        vm((c1, 8 * wide), BF),
        vm((9 * c2, 3 * c2), F32),
        vm((nxy, e_rows, LANES), BF),
        vm((nxy, e_rows, LANES), BF),
        vm((nxy, lr, LANES), F32),
        vm((nxy, lr, LANES), F32),
        vm((LANES + c1, LANES), F32),
        vm((nzg, zr, LANES), F32),
        vm((nzg, zr, LANES), F32),
        vm((zr, LANES), F32),
        vm((nzg, zr, LANES), F32),
        vm((e_rows, LANES), BF),
        vm((nxy, e_rows, LANES), BF),
        vm((lr, LANES), F32),
        vm((nxy, lr, LANES), F32),
        vm((nxy * e_rows, LANES), F32),
        dma((6,)), dma((6,)),
    ] + [dma] * 12
    shape = jax.ShapeDtypeStruct
    whole = pl.BlockSpec(memory_space=pltpu.VMEM)
    outs = pl.pallas_call(
        functools.partial(body, ns, nspace),
        out_shape=(
            shape(fields.shape, BF),
            shape((27, nf, c1), F32),
            shape((8, c1, c2), F32),
            shape((27, c2, c2), F32),
            shape((8, c1, c2), F32),
            shape((nf, c1), F32),
        ),
        in_specs=[whole] * 13,
        out_specs=[whole] * 6,
        scratch_shapes=scratch,
        compiler_params=pltpu.CompilerParams(
            collective_id=0, has_side_effects=True, vmem_limit_bytes=48 * 2**20
        ),
        name="unet_block",
    )(
        fields, cotangent, w_in.transpose(0, 2, 1), w_down.transpose(0, 2, 1), w_coarse, w_up,
        w_out, *consts,
    )
    prediction, g_in, g_dn, g_co, g_up, g_out = outs
    return (prediction, g_in.transpose(0, 2, 1), g_dn.transpose(0, 2, 1), g_co, g_up, g_out)


def solution(mesh):
    split = P("sample", None, "space", None, None)
    return jax.shard_map(
        shards,
        mesh=mesh,
        in_specs=(split, split, P(), P(), P(), P(), P()),
        out_specs=(split, P(), P(), P(), P(), P()),
        check_vma=False,
    )
```

```python
import functools

import jax
import jax.numpy as jnp
import numpy as np
from jax import lax
from jax.experimental import pallas as pl
from jax.experimental.pallas import tpu as pltpu
from jax.sharding import PartitionSpec as P

MESH = pl.DeviceIdType.MESH
BF = jnp.bfloat16
F32 = jnp.float32
LANES = 128
CHUNK = 256
VMEM = 63 * 2**20
HIGH = 2


def dot(a, b):
    return lax.dot_general(a, b, (((1,), (0,)), ((), ())), preferred_element_type=F32)


def dot_nt(a, b):
    return lax.dot_general(a, b, (((1,), (1,)), ((), ())), preferred_element_type=F32)


def one_hots(ny, nz, nf):
    wide = nz // 2
    rows = (ny + 2) * 4 * nf
    perm = np.zeros((rows, 4 * nf * ny), np.float32)
    own = 2 * nf * ny
    for y in range(ny):
        for f in range(nf):
            for dx in range(4):
                if dx == 0:
                    source = own + f * ny + y
                elif dx == 3:
                    source = own + nf * ny + f * ny + y
                else:
                    source = (f * 2 + dx - 1) * ny + y
                perm[(y + 1) * 4 * nf + dx * nf + f, source] = 1
    perm2 = np.zeros((2 * nf * ny, 2 * nf * ny), np.float32)
    for y in range(ny):
        for x in range(2):
            for f in range(nf):
                perm2[y * 2 * nf + x * nf + f, (f * 2 + x) * ny + y] = 1
    split = np.zeros((nz, 4 * wide), np.float32)
    for d in range(4):
        for z in range(wide):
            if 0 <= 2 * z + d - 1 < nz:
                split[2 * z + d - 1, d * wide + z] = 1
    join = split[:, wide : 3 * wide].T.copy()
    fold = np.zeros((128, 8 * 64 * nf), np.float32)
    for m in range(8):
        mz, my, mx = m // 4, m // 2 % 2, m % 2
        for k in range(27):
            dx, dy, dz = k // 9 + mx, k // 3 % 3 + my, k % 3 + mz
            for c in range(nf):
                fold[k * nf + c, m * 64 * nf + (dy * 4 + dz) * 4 * nf + dx * nf + c] = 1
    return [jnp.asarray(v, BF) for v in (perm, perm2, perm2.T.copy(), split, join, fold)]


def part_of(m):
    return 4 * (m % 2) + 2 * (m // 2 % 2) + m // 4


def body(
    ns, nspace,
    *refs,
):
    given, results, inputs, rest = refs[:13], refs[13:19], refs[19:32], refs[32:]
    work(ns, nspace, given, results, inputs, *rest)


def work(
    ns, nspace, given, results, inputs,
    f_land, ff, tt, patches, win, win_t, wdt, wd, wu, wut, bd, bdt, wf, wb, wa,
    act, slope, cots, cot_t, bm, term, red, r_land, bc, b_land, rolled, act_c, pred_t, bf,
    red_out, bc_out,
    gi_wide, gc, e_rest, e_send, e_recv, l_send, l_recv, late, ez_out, ez_all, lz_out, lz_all,
    e_out, e_all, l_out, l_all, full,
    in_s, halo_ss, halo_rs,
    e_ss, e_rs, l_ss, l_rs, z_ss, z_rs, y_ss, y_rs, a_ss, a_rs, b_ss, b_rs,
):
    fields, cot, w_in, w_dn, w_co, w_up, w_out, perm, perm2, perm2t, split, join, fold = inputs
    pred, g_in, g_dn, g_co, g_up, g_out = results
    nzg = nspace // HIGH
    nxy = ns * HIGH
    s = lax.axis_index("sample")
    sp = lax.axis_index("space")
    high, zi = sp // nzg, lax.rem(sp, nzg)
    me = high * ns + s
    left = lax.rem(sp + nspace - 1, nspace)
    right = lax.rem(sp + 1, nspace)
    has_left = jnp.where(sp > 0, 1.0, 0.0).astype(F32)
    has_right = jnp.where(sp < nspace - 1, 1.0, 0.0).astype(F32)

    def plane_peer(i):
        peer = lax.rem(me + i, nxy)
        return peer, (lax.rem(peer, ns), (peer // ns) * nzg + zi)

    def z_peer(i):
        peer = lax.rem(zi + i, nzg)
        return peer, (s, high * nzg + peer)

    barrier = pltpu.get_barrier_semaphore()

    def greet(device):
        pl.semaphore_signal(barrier, inc=1, device_id=device, device_id_type=MESH)

    def greet_plane(i, carry):
        greet(plane_peer(i)[1])
        return carry

    def greet_far(i, carry):
        greet(z_peer(nzg // 2 + i)[1])
        greet(z_peer(nzg // 2 - i)[1])
        return carry

    greet(z_peer(nzg // 2)[1])
    lax.fori_loop(1, nzg // 2, greet_far, 0)
    lax.fori_loop(1, nxy, greet_plane, 0)
    greet((s, left))
    greet((s, right))
    loads = [
        pltpu.make_async_copy(src, dst, in_s.at[i])
        for i, (src, dst) in enumerate(zip(given, inputs))
    ]
    for i in (0, 2, 12, 3, 5, 6, 4, 1, 8, 10, 7, 9, 11):
        loads[i].start()
    loads[0].wait()
    pl.semaphore_wait(barrier, 2 + nxy - 1 + nzg - 1)

    def halo(step, to_left, to_right, from_left, from_right):
        copies = [
            pltpu.make_async_remote_copy(
                src_ref=to_right, dst_ref=from_left, send_sem=halo_ss.at[2 * step],
                recv_sem=halo_rs.at[2 * step], device_id=(s, right), device_id_type=MESH,
            ),
            pltpu.make_async_remote_copy(
                src_ref=to_left, dst_ref=from_right, send_sem=halo_ss.at[2 * step + 1],
                recv_sem=halo_rs.at[2 * step + 1], device_id=(s, left), device_id_type=MESH,
            ),
        ]
        for copy in copies:
            copy.start()
        return copies

    def finish(copies):
        for copy in copies:
            copy.wait()

    nf, ny, nz = fields.shape[1], fields.shape[3], fields.shape[4]
    c1, c2 = w_up.shape[1], w_up.shape[2]
    yc = ny // 2
    cells = yc * LANES
    chunks = cells // CHUNK
    fr = 4 * nf
    hr = 2 * nf

    def halo_chunk(step, n, src, land):
        at = pl.ds(n * CHUNK, CHUNK)
        return halo(
            step * chunks + n + 1, src.at[:, at], src.at[:, at], land.at[0, :, at], land.at[1, :, at]
        )

    f_copies = halo(0, fields.at[0, :, 0], fields.at[0, :, 1], f_land.at[0], f_land.at[1])
    for i in (2, 12, 3, 5, 6, 4):
        loads[i].wait()

    win_t[...] = jnp.zeros_like(win_t)
    for k in range(27):
        win_t[k * nf : (k + 1) * nf, 0:c1] = w_in[k].astype(F32)
    flat = win_t[...].T[0:c1, :].astype(BF)
    spread_w = dot(flat, fold[...]).astype(BF)
    for m in range(8):
        win[m * c1 : (m + 1) * c1, :] = spread_w[:, m * 64 * nf : (m + 1) * 64 * nf]
        wdt[m * c1 : (m + 1) * c1, :] = w_dn[part_of(m)]
        wu[m * c1 : (m + 1) * c1, :] = w_up[part_of(m)]
    wd[...] = wdt[...].astype(F32).T.astype(BF)
    wut[...] = wu[...].astype(F32).T.astype(BF)
    bd[...] = jnp.zeros_like(bd)
    for m in range(8):
        bd[m * nf : (m + 1) * nf, m * c1 : (m + 1) * c1] = w_out[...].astype(F32)
    bdt[...] = bd[...].T.astype(BF)
    bd_b = bd[...].astype(BF)
    for q in range(3):
        for a in range(3):
            wf[q, :, a * c2 : (a + 1) * c2] = jnp.concatenate(
                [w_co[9 * a + 3 * q + b] for b in range(3)], axis=0
            ).astype(F32)
            for b in range(3):
                wa[q, a * c2 : (a + 1) * c2, b * c2 : (b + 1) * c2] = w_co[
                    9 * (2 - a) + 3 * (2 - q) + b
                ].astype(F32)
        wb[q] = wa[q].T.astype(BF)

    for i in (1, 8, 10, 7, 9, 11):
        loads[i].wait()
    cot_rows = cot[0].astype(F32).reshape(2 * nf * ny, nz).astype(BF)
    cot_t[...] = dot(dot(perm2[...], cot_rows).astype(BF), split[:, LANES : 3 * LANES]).astype(BF)
    for y in range(yc):
        for m in range(2):
            cots[m * 2 * hr : (m + 1) * 2 * hr, y * LANES : (y + 1) * LANES] = cot_t[
                y * 2 * hr : (y + 1) * 2 * hr, m * LANES : (m + 1) * LANES
            ]
    for n in range(chunks):
        at = slice(n * CHUNK, (n + 1) * CHUNK)
        back = dot(bdt[...], cots[:, at]).astype(BF)
        bm[:, at] = back
        term[:, at] = dot(wut[...], back)

    rows = nf * ny
    ff[0 : 2 * rows, :] = fields[0].astype(F32).reshape(2 * rows, nz).astype(BF)
    finish(f_copies)
    ff[2 * rows : 3 * rows, :] = (f_land[0].astype(F32).reshape(rows, nz) * has_left).astype(BF)
    ff[3 * rows : 4 * rows, :] = (f_land[1].astype(F32).reshape(rows, nz) * has_right).astype(BF)
    tt[...] = dot(dot(perm[...], ff[...]).astype(BF), split[...]).astype(BF)
    for y in range(yc):
        for dy in range(4):
            for dz in range(4):
                patches[(dy * 4 + dz) * fr : (dy * 4 + dz + 1) * fr, y * LANES : (y + 1) * LANES] = tt[
                    (2 * y + dy) * fr : (2 * y + dy + 1) * fr, dz * LANES : (dz + 1) * LANES
                ]
    r_copies = []
    for n in range(chunks):
        at = slice(n * CHUNK, (n + 1) * CHUNK)
        pre = dot(win[...], patches[:, at])
        sigma = jax.nn.sigmoid(pre)
        fine = (pre * sigma).astype(BF)
        slope[:, at] = sigma * (1.0 + pre * (1.0 - sigma))
        act[:, at] = fine
        red_out[:, at] = dot(wd[...], fine).astype(BF)
        r_copies.append(halo_chunk(0, n, red_out, r_land))
    edge = jnp.zeros((3 * c2, LANES), BF)
    for planes in (red, bc):
        planes[:, 0:LANES] = edge
        planes[:, LANES + cells : 2 * LANES + cells] = edge
    inner = slice(LANES, LANES + cells)
    red[c2 : 2 * c2, inner] = red_out[...]

    def arrive(n, copies, land, planes):
        finish(copies[n])
        at = slice(n * CHUNK, (n + 1) * CHUNK)
        there = slice(LANES + n * CHUNK, LANES + (n + 1) * CHUNK)
        planes[0:c2, there] = (land[0, :, at].astype(F32) * has_left).astype(BF)
        planes[2 * c2 : 3 * c2, there] = (land[1, :, at].astype(F32) * has_right).astype(BF)


    lane = lax.rem(lax.broadcasted_iota(jnp.int32, (c2, CHUNK), 1), LANES)
    not_first, not_last = lane > 0, lane < LANES - 1

    def later(v):
        return jnp.where(not_first, pltpu.roll(v, 1, 1), 0.0)

    def sooner(v):
        return jnp.where(not_last, pltpu.roll(v, CHUNK - 1, 1), 0.0)

    wf_b = [wf[q].astype(BF) for q in range(3)]

    b_copies = []
    arrive(0, r_copies, r_land, red)
    for n in range(chunks):
        if n + 1 < chunks:
            arrive(n + 1, r_copies, r_land, red)
        at = slice(n * CHUNK, (n + 1) * CHUNK)
        out = sum(
            dot(wf_b[q], red[:, n * CHUNK + q * LANES : (n + 1) * CHUNK + q * LANES])
            for q in range(3)
        )
        pre = out[c2 : 2 * c2] + later(out[0:c2]) + sooner(out[2 * c2 : 3 * c2])
        sigma = jax.nn.sigmoid(pre)
        act_c[:, at] = (pre * sigma).astype(BF)
        back = (term[:, at] * (sigma * (1.0 + pre * (1.0 - sigma)))).astype(BF)
        bc_out[:, at] = back
        b_copies.append(halo_chunk(1, n, bc_out, b_land))
        wide = back.astype(F32)
        rolled[0:c2, at] = sooner(wide).astype(BF)
        rolled[c2 : 2 * c2, at] = back
        rolled[2 * c2 : 3 * c2, at] = later(wide).astype(BF)
    bc[c2 : 2 * c2, inner] = bc_out[...]

    for q in range(3):
        gc[q * 3 * c2 : (q + 1) * 3 * c2, :] = dot_nt(
            rolled[...], red[:, q * LANES : q * LANES + cells]
        )
    def plane_copy(i, src, dst, send_sem, recv_sem):
        return pltpu.make_async_remote_copy(
            src_ref=src, dst_ref=dst, send_sem=send_sem, recv_sem=recv_sem,
            device_id=plane_peer(i)[1], device_id_type=MESH,
        )

    def send_early(h):
        def one(i, carry):
            plane_copy(
                i, e_send.at[h, plane_peer(i)[0]], e_recv.at[h, i], e_ss.at[h], e_rs.at[h]
            ).start()
            return carry

        lax.fori_loop(1, nxy, one, 0)
        e_recv[h, 0] = e_send[h, me]

    e_rows = e_send.shape[2]
    head = nxy * e_rows
    e_send[0] = gc[0:head, 0:LANES].astype(BF).reshape(nxy, e_rows, LANES)
    send_early(0)

    g_out_wide = jnp.zeros((8 * nf, 8 * c1), F32)
    for n in range(chunks):
        at = slice(n * CHUNK, (n + 1) * CHUNK)
        merged = (act[:, at].astype(F32) + dot(wu[...], act_c[:, at])).astype(BF)
        out = dot(bd_b, merged).astype(BF)
        g_out_wide = g_out_wide + dot_nt(cots[:, at], merged)
        for y in range(CHUNK // LANES):
            for m in range(2):
                pred_t[
                    (n * (CHUNK // LANES) + y) * 2 * hr : (n * (CHUNK // LANES) + y + 1) * 2 * hr,
                    m * LANES : (m + 1) * LANES,
                ] = out[m * 2 * hr : (m + 1) * 2 * hr, y * LANES : (y + 1) * LANES]
    gu = dot_nt(bm[...], act_c[...])
    mine = (
        lax.broadcasted_iota(jnp.int32, (8 * nf, 8 * c1), 0) // nf
        == lax.broadcasted_iota(jnp.int32, (8 * nf, 8 * c1), 1) // c1
    )
    g_out_wide = jnp.where(mine, g_out_wide, 0.0)
    g_out_half = g_out_wide[:, 0:LANES] + g_out_wide[:, LANES : 2 * LANES]
    g_out_half = g_out_half + pltpu.roll(g_out_half, 64, 1)
    g_out_half = g_out_half + pltpu.roll(g_out_half, 32, 1)
    g_out_half = g_out_half[0:8] + g_out_half[8:16] + g_out_half[16:24] + g_out_half[24:32]
    g_out_half = g_out_half + pltpu.roll(g_out_half, 4, 0)

    half = 9 * c2 // 2
    tail = 9 * c2 - head
    e_rest[0:tail, :] = gc[head:, 0:LANES].astype(BF)
    e_rest[tail : tail + half, 0:c2] = gc[0:half, LANES : LANES + c2].astype(BF)
    e_rest[tail : tail + half, c2 : 2 * c2] = gc[half : 2 * half, LANES : LANES + c2].astype(BF)
    up_at = tail + half
    e_rest[up_at : up_at + LANES, 0:c2] = gu[0:LANES].astype(BF)
    e_rest[up_at : up_at + LANES, c2 : 2 * c2] = gu[LANES : 2 * LANES].astype(BF)
    out_at = up_at + LANES
    e_rest[out_at : out_at + 32, :] = jnp.concatenate(
        [g_out_half, jnp.zeros((24, LANES), F32)], axis=0
    ).astype(BF)
    e_send[1] = e_rest[...].reshape(nxy, e_rows, LANES)
    send_early(1)

    arrive(0, b_copies, b_land, bc)
    for n in range(chunks):
        if n + 1 < chunks:
            arrive(n + 1, b_copies, b_land, bc)
        at = slice(n * CHUNK, (n + 1) * CHUNK)
        out = sum(
            dot(wb[q], bc[:, n * CHUNK + q * LANES : (n + 1) * CHUNK + q * LANES])
            for q in range(3)
        )
        back = out[c2 : 2 * c2] + sooner(out[0:c2]) + later(out[2 * c2 : 3 * c2])
        back = back.astype(BF)
        bc_out_at = rolled
        bc_out_at[0:c2, at] = back
        bf[:, at] = ((bm[:, at].astype(F32) + dot(wdt[...], back)) * slope[:, at]).astype(BF)
    gd = dot_nt(act[...], rolled[0:c2, :])
    late[0:LANES, 0:c2] = gd[0:LANES]
    late[0:LANES, c2 : 2 * c2] = gd[LANES : 2 * LANES]
    gi = dot_nt(bf[...], patches[...]).astype(BF)
    for m in range(8):
        gi_wide[:, m * 64 * nf : (m + 1) * 64 * nf] = gi[m * c1 : (m + 1) * c1, :]
    late[LANES : LANES + c1, :] = dot_nt(gi_wide[...], fold[...])
    l_rows = (LANES + c1) // nxy
    for p in range(nxy):
        l_send[p, 0:l_rows, :] = late[p * l_rows : (p + 1) * l_rows, :]

    def send_late(i, carry):
        plane_copy(i, l_send.at[plane_peer(i)[0], 0:l_rows], l_recv.at[i, 0:l_rows], l_ss, l_rs).start()
        return carry

    lax.fori_loop(1, nxy, send_late, 0)
    l_recv[0, 0:l_rows, :] = l_send[me, 0:l_rows, :]

    def all_of(ref, sem, count, rows=None):
        block = ref.at[pl.ds(0, count)] if rows is None else ref.at[pl.ds(0, count), 0:rows]
        pltpu.make_async_copy(block, block, sem).wait()

    def send_z(src, dst, send_sem, recv_sem):
        def one(i, carry):
            pltpu.make_async_remote_copy(
                src_ref=src, dst_ref=dst, send_sem=send_sem, recv_sem=recv_sem,
                device_id=z_peer(i)[1], device_id_type=MESH,
            ).start()
            return carry

        lax.fori_loop(1, nzg, one, 0)

    def send_plane(src, dst, send_sem, recv_sem):
        def one(i, carry):
            plane_copy(i, src, dst, send_sem, recv_sem).start()
            return carry

        lax.fori_loop(1, nxy, one, 0)

    def early_z(h):
        all_of(e_recv.at[h], e_rs.at[h], nxy - 1)
        part = jnp.sum(e_recv[h].astype(F32), axis=0).astype(BF)
        ez_out[h] = part
        ez_all[h, zi] = part
        send_z(ez_out.at[h], ez_all.at[h, zi], z_ss.at[h], z_rs.at[h])

    def early_back(h):
        all_of(ez_all.at[h], z_rs.at[h], nzg - 1)
        part = jnp.sum(ez_all[h].astype(F32), axis=0).astype(BF)
        e_out[h] = part
        e_all[h, me] = part
        send_plane(e_out.at[h], e_all.at[h, me], a_ss.at[h], a_rs.at[h])

    early_z(0)
    early_z(1)

    out = dot(dot(perm2t[...], pred_t[...]).astype(BF), join[...])
    pred[0] = out.reshape(nf, 2, ny, nz).astype(BF)

    all_of(l_recv, l_rs, nxy - 1, l_rows)
    part = jnp.sum(l_recv[:, 0:l_rows, :], axis=0)
    lz_out[0:l_rows, :] = part
    lz_all[zi, 0:l_rows, :] = part
    send_z(lz_out.at[0:l_rows], lz_all.at[zi, 0:l_rows], y_ss, y_rs)

    early_back(0)
    early_back(1)

    all_of(lz_all, y_rs, nzg - 1, l_rows)
    part = jnp.sum(lz_all[:, 0:l_rows, :], axis=0)
    l_out[0:l_rows, :] = part
    l_all[me, 0:l_rows, :] = part
    send_plane(l_out.at[0:l_rows], l_all.at[me, 0:l_rows], b_ss, b_rs)

    all_of(l_send, l_ss, nxy - 1, l_rows)
    all_of(lz_all, y_ss, nzg - 1, l_rows)
    for h in range(2):
        all_of(e_send.at[h], e_ss.at[h], nxy - 1)
        all_of(ez_all.at[h], z_ss.at[h], nzg - 1)
        all_of(e_all.at[h], a_rs.at[h], nxy - 1)
    full[0:head, :] = e_all[0].astype(F32).reshape(head, LANES)
    full[head : 2 * head, :] = e_all[1].astype(F32).reshape(head, LANES)
    for n in range(9):
        block = full[n * c2 : (n + 1) * c2, :]
        g_co[n] = block[:, 0:c2]
        g_co[9 + n] = pltpu.roll(block, c2, 1)[:, 0:c2]
    for n in range(9):
        row = 9 * c2 + (n * c2) % half
        lo = min(c2, half - (n * c2) % half)
        block = full[row : row + lo, :]
        if n * c2 // half == 1:
            block = pltpu.roll(block, c2, 1)
        g_co[18 + n, 0:lo, :] = block[:, 0:c2]
        if lo < c2:
            rest = pltpu.roll(full[9 * c2 : 9 * c2 + c2 - lo, :], c2, 1)
            g_co[18 + n, lo:c2, :] = rest[:, 0:c2]
    up_at, out_at = head + up_at, head + out_at
    for m in range(4):
        block = full[up_at + m * c1 : up_at + (m + 1) * c1, :]
        g_up[part_of(m)] = block[:, 0:c2]
        g_up[part_of(m + 4)] = pltpu.roll(block, c2, 1)[:, 0:c2]
    g_out[...] = full[out_at : out_at + nf, 0:c1]
    all_of(l_all, b_rs, nxy - 1, l_rows)
    for p in range(nxy):
        late[p * l_rows : (p + 1) * l_rows, :] = l_all[p, 0:l_rows, :]
    for m in range(4):
        block = late[m * c1 : (m + 1) * c1, :]
        g_dn[part_of(m)] = block[:, 0:c2]
        g_dn[part_of(m + 4)] = pltpu.roll(block, c2, 1)[:, 0:c2]
    win_t[0:c1, :] = late[LANES : LANES + c1, :]
    flipped = win_t[...].T
    for k in range(27):
        g_in[k] = flipped[k * nf : (k + 1) * nf, 0:c1]
    for h in range(2):
        all_of(e_all.at[h], a_ss.at[h], nxy - 1)
    all_of(l_all, b_ss, nxy - 1, l_rows)


def leave(*refs):
    count = len(refs) // 2
    for i in range(count):
        refs[count + i][...] = refs[i][...]


def shards(fields, cotangent, w_in, w_down, w_coarse, w_up, w_out):
    ns, nspace = lax.axis_size("sample"), lax.axis_size("space")
    nf, ny, nz = fields.shape[1], fields.shape[3], fields.shape[4]
    c1, c2 = w_up.shape[1], w_up.shape[2]
    cells = (ny // 2) * (nz // 2)
    nxy, nzg = ns * HIGH, nspace // HIGH
    e_rows = (9 * c2 * 3 // 2 + LANES + 32) // (2 * nxy)
    l_rows = (LANES + c1) // nxy
    lr = -(-l_rows // 8) * 8
    wide = 64 * nf
    consts = one_hots(ny, nz, nf)
    vm = pltpu.VMEM
    dma = pltpu.SemaphoreType.DMA
    given = (
        fields, cotangent, w_in.transpose(0, 2, 1), w_down.transpose(0, 2, 1), w_coarse, w_up,
        w_out, *consts,
    )
    scratch = [vm(v.shape, v.dtype) for v in given] + [
        vm((2, nf, ny, nz), BF),
        vm((4 * nf * ny, nz), BF),
        vm(((ny + 2) * 4 * nf, 4 * LANES), BF),
        vm((wide, cells), BF),
        vm((8 * c1, wide), BF),
        vm((128, 128), F32),
        vm((8 * c1, c2), BF),
        vm((c2, 8 * c1), BF),
        vm((8 * c1, c2), BF),
        vm((c2, 8 * c1), BF),
        vm((8 * nf, 8 * c1), F32),
        vm((8 * c1, 8 * nf), BF),
        vm((3, 3 * c2, 3 * c2), F32),
        vm((3, 3 * c2, 3 * c2), BF),
        vm((3, 3 * c2, 3 * c2), F32),
        vm((8 * c1, cells), BF),
        vm((8 * c1, cells), F32),
        vm((8 * nf, cells), BF),
        vm((2 * nf * ny, 2 * LANES), BF),
        vm((8 * c1, cells), BF),
        vm((c2, cells), F32),
        vm((3 * c2, cells + 2 * LANES), BF),
        vm((2, c2, cells), BF),
        vm((3 * c2, cells + 2 * LANES), BF),
        vm((2, c2, cells), BF),
        vm((3 * c2, cells), BF),
        vm((c2, cells), BF),
        vm((2 * nf * ny, 2 * LANES), BF),
        vm((8 * c1, cells), BF),
        vm((c2, cells), BF),
        vm((c2, cells), BF),
        vm((c1, 8 * wide), BF),
        vm((9 * c2, 3 * c2), F32),
        vm((nxy * e_rows, LANES), BF),
        vm((2, nxy, e_rows, LANES), BF),
        vm((2, nxy, e_rows, LANES), BF),
        vm((nxy, lr, LANES), F32),
        vm((nxy, lr, LANES), F32),
        vm((LANES + c1, LANES), F32),
        vm((2, e_rows, LANES), BF),
        vm((2, nzg, e_rows, LANES), BF),
        vm((lr, LANES), F32),
        vm((nzg, lr, LANES), F32),
        vm((2, e_rows, LANES), BF),
        vm((2, nxy, e_rows, LANES), BF),
        vm((lr, LANES), F32),
        vm((nxy, lr, LANES), F32),
        vm((2 * nxy * e_rows, LANES), F32),
        dma((13,)), dma((2 + 4 * cells // CHUNK,)), dma((2 + 4 * cells // CHUNK,)),
        dma((2,)), dma((2,)), dma, dma, dma((2,)), dma((2,)), dma, dma, dma((2,)), dma((2,)), dma, dma,
    ]
    shape = jax.ShapeDtypeStruct
    whole = pl.BlockSpec(memory_space=pltpu.VMEM)
    far = pl.BlockSpec(memory_space=pltpu.HBM)
    shapes = (
        shape(fields.shape, BF),
        shape((27, nf, c1), F32),
        shape((8, c1, c2), F32),
        shape((27, c2, c2), F32),
        shape((8, c1, c2), F32),
        shape((nf, c1), F32),
    )
    outs = pl.pallas_call(
        functools.partial(body, ns, nspace),
        out_shape=shapes,
        in_specs=[far] * 13,
        out_specs=[whole] * 6,
        scratch_shapes=scratch,
        compiler_params=pltpu.CompilerParams(
            collective_id=0, has_side_effects=True, vmem_limit_bytes=VMEM
        ),
        name="unet_block",
    )(*given)
    outs = pl.pallas_call(
        leave,
        out_shape=shapes,
        in_specs=[whole] * 6,
        out_specs=[whole] * 6,
        compiler_params=pltpu.CompilerParams(vmem_limit_bytes=VMEM),
        name="leave",
    )(*outs)
    prediction, g_in, g_dn, g_co, g_up, g_out = outs
    return (prediction, g_in.transpose(0, 2, 1), g_dn.transpose(0, 2, 1), g_co, g_up, g_out)


def solution(mesh):
    split = P("sample", None, "space", None, None)
    return jax.shard_map(
        shards,
        mesh=mesh,
        in_specs=(split, split, P(), P(), P(), P(), P()),
        out_specs=(split, P(), P(), P(), P(), P()),
        check_vma=False,
    )
```

```python
import functools

import jax
import jax.numpy as jnp
import numpy as np
from jax import lax
from jax.experimental import pallas as pl
from jax.experimental.pallas import tpu as pltpu
from jax.sharding import PartitionSpec as P

MESH = pl.DeviceIdType.MESH
BF = jnp.bfloat16
F32 = jnp.float32
LANES = 128
CHUNK = 256
VMEM = 63 * 2**20
HIGH = 2


def dot(a, b):
    return lax.dot_general(a, b, (((1,), (0,)), ((), ())), preferred_element_type=F32)


def dot_nt(a, b):
    return lax.dot_general(a, b, (((1,), (1,)), ((), ())), preferred_element_type=F32)


def one_hots(ny, nz, nf):
    wide = nz // 2
    rows = (ny + 2) * 4 * nf
    perm = np.zeros((rows, 4 * nf * ny), np.float32)
    own = 2 * nf * ny
    for y in range(ny):
        for f in range(nf):
            for dx in range(4):
                if dx == 0:
                    source = own + f * ny + y
                elif dx == 3:
                    source = own + nf * ny + f * ny + y
                else:
                    source = (f * 2 + dx - 1) * ny + y
                perm[(y + 1) * 4 * nf + dx * nf + f, source] = 1
    perm2 = np.zeros((2 * nf * ny, 2 * nf * ny), np.float32)
    for y in range(ny):
        for x in range(2):
            for f in range(nf):
                perm2[y * 2 * nf + x * nf + f, (f * 2 + x) * ny + y] = 1
    split = np.zeros((nz, 4 * wide), np.float32)
    for d in range(4):
        for z in range(wide):
            if 0 <= 2 * z + d - 1 < nz:
                split[2 * z + d - 1, d * wide + z] = 1
    join = split[:, wide : 3 * wide].T.copy()
    fold = np.zeros((128, 8 * 64 * nf), np.float32)
    for m in range(8):
        mz, my, mx = m // 4, m // 2 % 2, m % 2
        for k in range(27):
            dx, dy, dz = k // 9 + mx, k // 3 % 3 + my, k % 3 + mz
            for c in range(nf):
                fold[k * nf + c, m * 64 * nf + (dy * 4 + dz) * 4 * nf + dx * nf + c] = 1
    return [jnp.asarray(v, BF) for v in (perm, perm2, perm2.T.copy(), split, join, fold)]


def part_of(m):
    return 4 * (m % 2) + 2 * (m // 2 % 2) + m // 4


def body(
    ns, nspace,
    *refs,
):
    given, results, inputs, rest = refs[:13], refs[13:19], refs[19:32], refs[32:]
    work(ns, nspace, given, results, inputs, *rest)


def work(
    ns, nspace, given, results, inputs,
    f_land, ff, tt, patches, win, win_t, wdt, wd, wu, wut, bd, bdt, wf, wb, wa,
    act, slope, cots, cot_t, bm, term, red, r_land, bc, b_land, rolled, act_c, pred_t, bf,
    red_out, bc_out,
    gi_wide, gc, e_rest, e_send, e_recv, l_send, l_recv, late, ez_out, ez_all, lz_out, lz_all,
    e_out, e_all, l_out, l_all, full,
    near_p, near_z, wide_p, wide_z, in_s, halo_ss, halo_rs,
    e_ss, e_rs, l_ss, l_rs, z_ss, z_rs, y_ss, y_rs, a_ss, a_rs, b_ss, b_rs,
):
    fields, cot, w_in, w_dn, w_co, w_up, w_out, perm, perm2, perm2t, split, join, fold = inputs
    pred, g_in, g_dn, g_co, g_up, g_out = results
    nzg = nspace // HIGH
    nxy = ns * HIGH
    s = lax.axis_index("sample")
    sp = lax.axis_index("space")
    high, zi = sp // nzg, lax.rem(sp, nzg)
    me = high * ns + s
    left = lax.rem(sp + nspace - 1, nspace)
    right = lax.rem(sp + 1, nspace)
    has_left = jnp.where(sp > 0, 1.0, 0.0).astype(F32)
    has_right = jnp.where(sp < nspace - 1, 1.0, 0.0).astype(F32)

    def plane_peer(i):
        peer = lax.rem(me + i, nxy)
        return peer, (lax.rem(peer, ns), (peer // ns) * nzg + zi)

    def z_peer(i):
        peer = lax.rem(zi + i, nzg)
        return peer, (s, high * nzg + peer)

    barrier = pltpu.get_barrier_semaphore()

    def greet(device):
        pl.semaphore_signal(barrier, inc=1, device_id=device, device_id_type=MESH)

    xs, pair = s // 4, lax.rem(s, 4)
    mates = [xs * 4 + lax.rem(pair + i, 4) for i in (1, 2, 3)]
    ring = [lax.rem(xs + i, ns // 4) * 4 + pair for i in range(1, ns // 4)]

    def along_z(i):
        return (s, high * nzg + lax.rem(zi + i + nzg, nzg))

    opposite = (s, (1 - high) * nzg + zi)
    greeted = [(s, left), (s, right), opposite]
    greeted += [(mate, sp) for mate in mates] + [(other, sp) for other in ring]
    greeted += [along_z(i) for i in (1, -1, 2, -2)]
    for device in greeted:
        greet(device)

    def tell(sem, devices):
        for device in devices:
            pl.semaphore_signal(sem, inc=1, device_id=device, device_id_type=MESH)

    loads = [
        pltpu.make_async_copy(src, dst, in_s.at[i])
        for i, (src, dst) in enumerate(zip(given, inputs))
    ]
    for i in (0, 2, 12, 3, 5, 6, 4, 1, 8, 10, 7, 9, 11):
        loads[i].start()
    loads[0].wait()
    pl.semaphore_wait(barrier, len(greeted))

    def halo(step, to_left, to_right, from_left, from_right):
        copies = [
            pltpu.make_async_remote_copy(
                src_ref=to_right, dst_ref=from_left, send_sem=halo_ss.at[2 * step],
                recv_sem=halo_rs.at[2 * step], device_id=(s, right), device_id_type=MESH,
            ),
            pltpu.make_async_remote_copy(
                src_ref=to_left, dst_ref=from_right, send_sem=halo_ss.at[2 * step + 1],
                recv_sem=halo_rs.at[2 * step + 1], device_id=(s, left), device_id_type=MESH,
            ),
        ]
        for copy in copies:
            copy.start()
        return copies

    def finish(copies):
        for copy in copies:
            copy.wait()

    nf, ny, nz = fields.shape[1], fields.shape[3], fields.shape[4]
    c1, c2 = w_up.shape[1], w_up.shape[2]
    yc = ny // 2
    cells = yc * LANES
    chunks = cells // CHUNK
    fr = 4 * nf
    hr = 2 * nf

    def halo_chunk(step, n, src, land):
        return halo(
            step * chunks + n + 1, src.at[n], src.at[n], land.at[0, n], land.at[1, n]
        )

    f_copies = halo(0, fields.at[0, :, 0], fields.at[0, :, 1], f_land.at[0], f_land.at[1])
    tell(near_p, [(mate, sp) for mate in mates])
    tell(near_z, [along_z(2), along_z(-2)])
    for i in (2, 12, 3, 5, 6, 4):
        loads[i].wait()

    win_t[...] = jnp.zeros_like(win_t)
    for k in range(27):
        win_t[k * nf : (k + 1) * nf, 0:c1] = w_in[k].astype(F32)
    flat = win_t[...].T[0:c1, :].astype(BF)
    spread_w = dot(flat, fold[...]).astype(BF)
    for m in range(8):
        win[m * c1 : (m + 1) * c1, :] = spread_w[:, m * 64 * nf : (m + 1) * 64 * nf]
        wdt[m * c1 : (m + 1) * c1, :] = w_dn[part_of(m)]
        wu[m * c1 : (m + 1) * c1, :] = w_up[part_of(m)]
    wd[...] = wdt[...].astype(F32).T.astype(BF)
    wut[...] = wu[...].astype(F32).T.astype(BF)
    bd[...] = jnp.zeros_like(bd)
    for m in range(8):
        bd[m * nf : (m + 1) * nf, m * c1 : (m + 1) * c1] = w_out[...].astype(F32)
    bdt[...] = bd[...].T.astype(BF)
    bd_b = bd[...].astype(BF)
    for q in range(3):
        for a in range(3):
            wf[q, :, a * c2 : (a + 1) * c2] = jnp.concatenate(
                [w_co[9 * a + 3 * q + b] for b in range(3)], axis=0
            ).astype(F32)
            for b in range(3):
                wa[q, a * c2 : (a + 1) * c2, b * c2 : (b + 1) * c2] = w_co[
                    9 * (2 - a) + 3 * (2 - q) + b
                ].astype(F32)
        wb[q] = wa[q].T.astype(BF)

    for i in (1, 8, 10, 7, 9, 11):
        loads[i].wait()
    cot_rows = cot[0].astype(F32).reshape(2 * nf * ny, nz).astype(BF)
    cot_t[...] = dot(dot(perm2[...], cot_rows).astype(BF), split[:, LANES : 3 * LANES]).astype(BF)
    for y in range(yc):
        for m in range(2):
            cots[m * 2 * hr : (m + 1) * 2 * hr, y * LANES : (y + 1) * LANES] = cot_t[
                y * 2 * hr : (y + 1) * 2 * hr, m * LANES : (m + 1) * LANES
            ]
    for n in range(chunks):
        at = slice(n * CHUNK, (n + 1) * CHUNK)
        back = dot(bdt[...], cots[:, at]).astype(BF)
        bm[:, at] = back
        term[:, at] = dot(wut[...], back)

    rows = nf * ny
    ff[0 : 2 * rows, :] = fields[0].astype(F32).reshape(2 * rows, nz).astype(BF)
    finish(f_copies)
    pl.semaphore_wait(near_p, 3)
    tell(wide_p, [opposite])
    pl.semaphore_wait(near_z, 2)
    tell(wide_z, [along_z(4), along_z(-4)])
    ff[2 * rows : 3 * rows, :] = (f_land[0].astype(F32).reshape(rows, nz) * has_left).astype(BF)
    ff[3 * rows : 4 * rows, :] = (f_land[1].astype(F32).reshape(rows, nz) * has_right).astype(BF)
    tt[...] = dot(dot(perm[...], ff[...]).astype(BF), split[...]).astype(BF)
    for y in range(yc):
        for dy in range(4):
            for dz in range(4):
                patches[(dy * 4 + dz) * fr : (dy * 4 + dz + 1) * fr, y * LANES : (y + 1) * LANES] = tt[
                    (2 * y + dy) * fr : (2 * y + dy + 1) * fr, dz * LANES : (dz + 1) * LANES
                ]
    r_copies = []
    for n in range(chunks):
        at = slice(n * CHUNK, (n + 1) * CHUNK)
        pre = dot(win[...], patches[:, at])
        sigma = jax.nn.sigmoid(pre)
        fine = (pre * sigma).astype(BF)
        slope[:, at] = sigma * (1.0 + pre * (1.0 - sigma))
        act[:, at] = fine
        down = dot(wd[...], fine).astype(BF)
        red_out[n] = down
        red[c2 : 2 * c2, LANES + n * CHUNK : LANES + (n + 1) * CHUNK] = down
        r_copies.append(halo_chunk(0, n, red_out, r_land))
    edge = jnp.zeros((3 * c2, LANES), BF)
    for planes in (red, bc):
        planes[:, 0:LANES] = edge
        planes[:, LANES + cells : 2 * LANES + cells] = edge

    def arrive(n, copies, land, planes):
        finish(copies[n])
        there = slice(LANES + n * CHUNK, LANES + (n + 1) * CHUNK)
        planes[0:c2, there] = (land[0, n].astype(F32) * has_left).astype(BF)
        planes[2 * c2 : 3 * c2, there] = (land[1, n].astype(F32) * has_right).astype(BF)


    lane = lax.rem(lax.broadcasted_iota(jnp.int32, (c2, CHUNK), 1), LANES)
    not_first, not_last = lane > 0, lane < LANES - 1

    def later(v):
        return jnp.where(not_first, pltpu.roll(v, 1, 1), 0.0)

    def sooner(v):
        return jnp.where(not_last, pltpu.roll(v, CHUNK - 1, 1), 0.0)

    wf_b = [wf[q].astype(BF) for q in range(3)]

    b_copies = []
    arrive(0, r_copies, r_land, red)
    for n in range(chunks):
        if n + 1 < chunks:
            arrive(n + 1, r_copies, r_land, red)
        at = slice(n * CHUNK, (n + 1) * CHUNK)
        out = sum(
            dot(wf_b[q], red[:, n * CHUNK + q * LANES : (n + 1) * CHUNK + q * LANES])
            for q in range(3)
        )
        pre = out[c2 : 2 * c2] + later(out[0:c2]) + sooner(out[2 * c2 : 3 * c2])
        sigma = jax.nn.sigmoid(pre)
        act_c[:, at] = (pre * sigma).astype(BF)
        back = (term[:, at] * (sigma * (1.0 + pre * (1.0 - sigma)))).astype(BF)
        bc_out[n] = back
        bc[c2 : 2 * c2, LANES + n * CHUNK : LANES + (n + 1) * CHUNK] = back
        b_copies.append(halo_chunk(1, n, bc_out, b_land))
        wide = back.astype(F32)
        rolled[0:c2, at] = sooner(wide).astype(BF)
        rolled[c2 : 2 * c2, at] = back
        rolled[2 * c2 : 3 * c2, at] = later(wide).astype(BF)

    for q in range(3):
        gc[q * 3 * c2 : (q + 1) * 3 * c2, :] = dot_nt(
            rolled[...], red[:, q * LANES : q * LANES + cells]
        )
    def plane_copy(i, src, dst, send_sem, recv_sem):
        return pltpu.make_async_remote_copy(
            src_ref=src, dst_ref=dst, send_sem=send_sem, recv_sem=recv_sem,
            device_id=plane_peer(i)[1], device_id_type=MESH,
        )

    def send_early(h):
        def one(i, carry):
            plane_copy(
                i, e_send.at[h, plane_peer(i)[0]], e_recv.at[h, i], e_ss.at[h], e_rs.at[h]
            ).start()
            return carry

        lax.fori_loop(1, nxy, one, 0)
        e_recv[h, 0] = e_send[h, me]

    e_rows = e_send.shape[2]
    head = nxy * e_rows
    pl.semaphore_wait(wide_p, 1)
    pl.semaphore_wait(wide_z, 2)
    e_send[0] = gc[0:head, 0:LANES].astype(BF).reshape(nxy, e_rows, LANES)
    send_early(0)

    g_out_wide = jnp.zeros((8 * nf, 8 * c1), F32)
    for n in range(chunks):
        at = slice(n * CHUNK, (n + 1) * CHUNK)
        merged = (act[:, at].astype(F32) + dot(wu[...], act_c[:, at])).astype(BF)
        out = dot(bd_b, merged).astype(BF)
        g_out_wide = g_out_wide + dot_nt(cots[:, at], merged)
        for y in range(CHUNK // LANES):
            for m in range(2):
                pred_t[
                    (n * (CHUNK // LANES) + y) * 2 * hr : (n * (CHUNK // LANES) + y + 1) * 2 * hr,
                    m * LANES : (m + 1) * LANES,
                ] = out[m * 2 * hr : (m + 1) * 2 * hr, y * LANES : (y + 1) * LANES]
    gu = dot_nt(bm[...], act_c[...])
    mine = (
        lax.broadcasted_iota(jnp.int32, (8 * nf, 8 * c1), 0) // nf
        == lax.broadcasted_iota(jnp.int32, (8 * nf, 8 * c1), 1) // c1
    )
    g_out_wide = jnp.where(mine, g_out_wide, 0.0)
    g_out_half = g_out_wide[:, 0:LANES] + g_out_wide[:, LANES : 2 * LANES]
    g_out_half = g_out_half + pltpu.roll(g_out_half, 64, 1)
    g_out_half = g_out_half + pltpu.roll(g_out_half, 32, 1)
    g_out_half = g_out_half[0:8] + g_out_half[8:16] + g_out_half[16:24] + g_out_half[24:32]
    g_out_half = g_out_half + pltpu.roll(g_out_half, 4, 0)

    half = 9 * c2 // 2
    tail = 9 * c2 - head
    e_rest[0:tail, :] = gc[head:, 0:LANES].astype(BF)
    e_rest[tail : tail + half, 0:c2] = gc[0:half, LANES : LANES + c2].astype(BF)
    e_rest[tail : tail + half, c2 : 2 * c2] = gc[half : 2 * half, LANES : LANES + c2].astype(BF)
    up_at = tail + half
    e_rest[up_at : up_at + LANES, 0:c2] = gu[0:LANES].astype(BF)
    e_rest[up_at : up_at + LANES, c2 : 2 * c2] = gu[LANES : 2 * LANES].astype(BF)
    out_at = up_at + LANES
    e_rest[out_at : out_at + 32, :] = jnp.concatenate(
        [g_out_half, jnp.zeros((24, LANES), F32)], axis=0
    ).astype(BF)
    e_send[1] = e_rest[...].reshape(nxy, e_rows, LANES)
    send_early(1)

    arrive(0, b_copies, b_land, bc)
    for n in range(chunks):
        if n + 1 < chunks:
            arrive(n + 1, b_copies, b_land, bc)
        at = slice(n * CHUNK, (n + 1) * CHUNK)
        out = sum(
            dot(wb[q], bc[:, n * CHUNK + q * LANES : (n + 1) * CHUNK + q * LANES])
            for q in range(3)
        )
        back = out[c2 : 2 * c2] + sooner(out[0:c2]) + later(out[2 * c2 : 3 * c2])
        back = back.astype(BF)
        bc_out_at = rolled
        bc_out_at[0:c2, at] = back
        bf[:, at] = ((bm[:, at].astype(F32) + dot(wdt[...], back)) * slope[:, at]).astype(BF)
    gd = dot_nt(act[...], rolled[0:c2, :])
    late[0:LANES, 0:c2] = gd[0:LANES]
    late[0:LANES, c2 : 2 * c2] = gd[LANES : 2 * LANES]
    gi = dot_nt(bf[...], patches[...]).astype(BF)
    for m in range(8):
        gi_wide[:, m * 64 * nf : (m + 1) * 64 * nf] = gi[m * c1 : (m + 1) * c1, :]
    late[LANES : LANES + c1, :] = dot_nt(gi_wide[...], fold[...])
    l_rows = (LANES + c1) // nxy
    for p in range(nxy):
        l_send[p, 0:l_rows, :] = late[p * l_rows : (p + 1) * l_rows, :]

    def send_late(i, carry):
        plane_copy(i, l_send.at[plane_peer(i)[0], 0:l_rows], l_recv.at[i, 0:l_rows], l_ss, l_rs).start()
        return carry

    lax.fori_loop(1, nxy, send_late, 0)
    l_recv[0, 0:l_rows, :] = l_send[me, 0:l_rows, :]

    def all_of(ref, sem, count, rows=None):
        block = ref.at[pl.ds(0, count)] if rows is None else ref.at[pl.ds(0, count), 0:rows]
        pltpu.make_async_copy(block, block, sem).wait()

    def send_z(src, dst, send_sem, recv_sem):
        def one(i, carry):
            pltpu.make_async_remote_copy(
                src_ref=src, dst_ref=dst, send_sem=send_sem, recv_sem=recv_sem,
                device_id=z_peer(i)[1], device_id_type=MESH,
            ).start()
            return carry

        lax.fori_loop(1, nzg, one, 0)

    def send_plane(src, dst, send_sem, recv_sem):
        def one(i, carry):
            plane_copy(i, src, dst, send_sem, recv_sem).start()
            return carry

        lax.fori_loop(1, nxy, one, 0)

    def early_z(h):
        all_of(e_recv.at[h], e_rs.at[h], nxy - 1)
        part = jnp.sum(e_recv[h].astype(F32), axis=0).astype(BF)
        ez_out[h] = part
        ez_all[h, zi] = part
        send_z(ez_out.at[h], ez_all.at[h, zi], z_ss.at[h], z_rs.at[h])

    def early_back(h):
        all_of(ez_all.at[h], z_rs.at[h], nzg - 1)
        part = jnp.sum(ez_all[h].astype(F32), axis=0).astype(BF)
        e_out[h] = part
        e_all[h, me] = part
        send_plane(e_out.at[h], e_all.at[h, me], a_ss.at[h], a_rs.at[h])

    early_z(0)
    early_z(1)

    out = dot(dot(perm2t[...], pred_t[...]).astype(BF), join[...])
    pred[0] = out.reshape(nf, 2, ny, nz).astype(BF)

    all_of(l_recv, l_rs, nxy - 1, l_rows)
    part = jnp.sum(l_recv[:, 0:l_rows, :], axis=0)
    lz_out[0:l_rows, :] = part
    lz_all[zi, 0:l_rows, :] = part
    send_z(lz_out.at[0:l_rows], lz_all.at[zi, 0:l_rows], y_ss, y_rs)

    early_back(0)
    early_back(1)

    all_of(lz_all, y_rs, nzg - 1, l_rows)
    part = jnp.sum(lz_all[:, 0:l_rows, :], axis=0)
    l_out[0:l_rows, :] = part
    l_all[me, 0:l_rows, :] = part
    send_plane(l_out.at[0:l_rows], l_all.at[me, 0:l_rows], b_ss, b_rs)

    all_of(l_send, l_ss, nxy - 1, l_rows)
    all_of(lz_all, y_ss, nzg - 1, l_rows)
    for h in range(2):
        all_of(e_send.at[h], e_ss.at[h], nxy - 1)
        all_of(ez_all.at[h], z_ss.at[h], nzg - 1)
        all_of(e_all.at[h], a_rs.at[h], nxy - 1)
    full[0:head, :] = e_all[0].astype(F32).reshape(head, LANES)
    full[head : 2 * head, :] = e_all[1].astype(F32).reshape(head, LANES)
    for n in range(9):
        block = full[n * c2 : (n + 1) * c2, :]
        g_co[n] = block[:, 0:c2]
        g_co[9 + n] = pltpu.roll(block, c2, 1)[:, 0:c2]
    for n in range(9):
        row = 9 * c2 + (n * c2) % half
        lo = min(c2, half - (n * c2) % half)
        block = full[row : row + lo, :]
        if n * c2 // half == 1:
            block = pltpu.roll(block, c2, 1)
        g_co[18 + n, 0:lo, :] = block[:, 0:c2]
        if lo < c2:
            rest = pltpu.roll(full[9 * c2 : 9 * c2 + c2 - lo, :], c2, 1)
            g_co[18 + n, lo:c2, :] = rest[:, 0:c2]
    up_at, out_at = head + up_at, head + out_at
    for m in range(4):
        block = full[up_at + m * c1 : up_at + (m + 1) * c1, :]
        g_up[part_of(m)] = block[:, 0:c2]
        g_up[part_of(m + 4)] = pltpu.roll(block, c2, 1)[:, 0:c2]
    g_out[...] = full[out_at : out_at + nf, 0:c1]
    all_of(l_all, b_rs, nxy - 1, l_rows)
    for p in range(nxy):
        late[p * l_rows : (p + 1) * l_rows, :] = l_all[p, 0:l_rows, :]
    for m in range(4):
        block = late[m * c1 : (m + 1) * c1, :]
        g_dn[part_of(m)] = block[:, 0:c2]
        g_dn[part_of(m + 4)] = pltpu.roll(block, c2, 1)[:, 0:c2]
    win_t[0:c1, :] = late[LANES : LANES + c1, :]
    flipped = win_t[...].T
    for k in range(27):
        g_in[k] = flipped[k * nf : (k + 1) * nf, 0:c1]
    for h in range(2):
        all_of(e_all.at[h], a_ss.at[h], nxy - 1)
    all_of(l_all, b_ss, nxy - 1, l_rows)


def leave(*refs):
    count = len(refs) // 2
    for i in range(count):
        refs[count + i][...] = refs[i][...]


def shards(fields, cotangent, w_in, w_down, w_coarse, w_up, w_out):
    ns, nspace = lax.axis_size("sample"), lax.axis_size("space")
    nf, ny, nz = fields.shape[1], fields.shape[3], fields.shape[4]
    c1, c2 = w_up.shape[1], w_up.shape[2]
    cells = (ny // 2) * (nz // 2)
    nxy, nzg = ns * HIGH, nspace // HIGH
    e_rows = (9 * c2 * 3 // 2 + LANES + 32) // (2 * nxy)
    l_rows = (LANES + c1) // nxy
    lr = -(-l_rows // 8) * 8
    wide = 64 * nf
    consts = one_hots(ny, nz, nf)
    vm = pltpu.VMEM
    dma = pltpu.SemaphoreType.DMA
    regular = pltpu.SemaphoreType.REGULAR
    given = (
        fields, cotangent, w_in.transpose(0, 2, 1), w_down.transpose(0, 2, 1), w_coarse, w_up,
        w_out, *consts,
    )
    scratch = [vm(v.shape, v.dtype) for v in given] + [
        vm((2, nf, ny, nz), BF),
        vm((4 * nf * ny, nz), BF),
        vm(((ny + 2) * 4 * nf, 4 * LANES), BF),
        vm((wide, cells), BF),
        vm((8 * c1, wide), BF),
        vm((128, 128), F32),
        vm((8 * c1, c2), BF),
        vm((c2, 8 * c1), BF),
        vm((8 * c1, c2), BF),
        vm((c2, 8 * c1), BF),
        vm((8 * nf, 8 * c1), F32),
        vm((8 * c1, 8 * nf), BF),
        vm((3, 3 * c2, 3 * c2), F32),
        vm((3, 3 * c2, 3 * c2), BF),
        vm((3, 3 * c2, 3 * c2), F32),
        vm((8 * c1, cells), BF),
        vm((8 * c1, cells), F32),
        vm((8 * nf, cells), BF),
        vm((2 * nf * ny, 2 * LANES), BF),
        vm((8 * c1, cells), BF),
        vm((c2, cells), F32),
        vm((3 * c2, cells + 2 * LANES), BF),
        vm((2, cells // CHUNK, c2, CHUNK), BF),
        vm((3 * c2, cells + 2 * LANES), BF),
        vm((2, cells // CHUNK, c2, CHUNK), BF),
        vm((3 * c2, cells), BF),
        vm((c2, cells), BF),
        vm((2 * nf * ny, 2 * LANES), BF),
        vm((8 * c1, cells), BF),
        vm((cells // CHUNK, c2, CHUNK), BF),
        vm((cells // CHUNK, c2, CHUNK), BF),
        vm((c1, 8 * wide), BF),
        vm((9 * c2, 3 * c2), F32),
        vm((nxy * e_rows, LANES), BF),
        vm((2, nxy, e_rows, LANES), BF),
        vm((2, nxy, e_rows, LANES), BF),
        vm((nxy, lr, LANES), F32),
        vm((nxy, lr, LANES), F32),
        vm((LANES + c1, LANES), F32),
        vm((2, e_rows, LANES), BF),
        vm((2, nzg, e_rows, LANES), BF),
        vm((lr, LANES), F32),
        vm((nzg, lr, LANES), F32),
        vm((2, e_rows, LANES), BF),
        vm((2, nxy, e_rows, LANES), BF),
        vm((lr, LANES), F32),
        vm((nxy, lr, LANES), F32),
        vm((2 * nxy * e_rows, LANES), F32),
        regular, regular, regular, regular, dma((13,)), dma((2 + 4 * cells // CHUNK,)), dma((2 + 4 * cells // CHUNK,)),
        dma((2,)), dma((2,)), dma, dma, dma((2,)), dma((2,)), dma, dma, dma((2,)), dma((2,)), dma, dma,
    ]
    shape = jax.ShapeDtypeStruct
    whole = pl.BlockSpec(memory_space=pltpu.VMEM)
    far = pl.BlockSpec(memory_space=pltpu.HBM)
    shapes = (
        shape(fields.shape, BF),
        shape((27, nf, c1), F32),
        shape((8, c1, c2), F32),
        shape((27, c2, c2), F32),
        shape((8, c1, c2), F32),
        shape((nf, c1), F32),
    )
    outs = pl.pallas_call(
        functools.partial(body, ns, nspace),
        out_shape=shapes,
        in_specs=[far] * 13,
        out_specs=[whole] * 6,
        scratch_shapes=scratch,
        compiler_params=pltpu.CompilerParams(
            collective_id=0, has_side_effects=True, vmem_limit_bytes=VMEM
        ),
        name="unet_block",
    )(*given)
    outs = pl.pallas_call(
        leave,
        out_shape=shapes,
        in_specs=[whole] * 6,
        out_specs=[whole] * 6,
        compiler_params=pltpu.CompilerParams(vmem_limit_bytes=VMEM),
        name="leave",
    )(*outs)
    prediction, g_in, g_dn, g_co, g_up, g_out = outs
    return (prediction, g_in.transpose(0, 2, 1), g_dn.transpose(0, 2, 1), g_co, g_up, g_out)


def solution(mesh):
    split = P("sample", None, "space", None, None)
    return jax.shard_map(
        shards,
        mesh=mesh,
        in_specs=(split, split, P(), P(), P(), P(), P()),
        out_specs=(split, P(), P(), P(), P(), P()),
        check_vma=False,
    )
```

```python
import functools

import jax
import jax.numpy as jnp
import numpy as np
from jax import lax
from jax.experimental import pallas as pl
from jax.experimental.pallas import tpu as pltpu
from jax.sharding import PartitionSpec as P

MESH = pl.DeviceIdType.MESH
BF = jnp.bfloat16
F32 = jnp.float32
LANES = 128
CHUNK = 256
VMEM = 63 * 2**20
HIGH = 2


def dot(a, b):
    return lax.dot_general(a, b, (((1,), (0,)), ((), ())), preferred_element_type=F32)


def dot_nt(a, b):
    return lax.dot_general(a, b, (((1,), (1,)), ((), ())), preferred_element_type=F32)


def one_hots(ny, nz, nf):
    wide = nz // 2
    rows = (ny + 2) * 4 * nf
    perm = np.zeros((rows, 4 * nf * ny), np.float32)
    own = 2 * nf * ny
    for y in range(ny):
        for f in range(nf):
            for dx in range(4):
                if dx == 0:
                    source = own + f * ny + y
                elif dx == 3:
                    source = own + nf * ny + f * ny + y
                else:
                    source = (f * 2 + dx - 1) * ny + y
                perm[(y + 1) * 4 * nf + dx * nf + f, source] = 1
    perm2 = np.zeros((2 * nf * ny, 2 * nf * ny), np.float32)
    for y in range(ny):
        for x in range(2):
            for f in range(nf):
                perm2[y * 2 * nf + x * nf + f, (f * 2 + x) * ny + y] = 1
    split = np.zeros((nz, 4 * wide), np.float32)
    for d in range(4):
        for z in range(wide):
            if 0 <= 2 * z + d - 1 < nz:
                split[2 * z + d - 1, d * wide + z] = 1
    join = split[:, wide : 3 * wide].T.copy()
    fold = np.zeros((128, 8 * 64 * nf), np.float32)
    for m in range(8):
        mz, my, mx = m // 4, m // 2 % 2, m % 2
        for k in range(27):
            dx, dy, dz = k // 9 + mx, k // 3 % 3 + my, k % 3 + mz
            for c in range(nf):
                fold[k * nf + c, m * 64 * nf + (dy * 4 + dz) * 4 * nf + dx * nf + c] = 1
    return [jnp.asarray(v, BF) for v in (perm, perm2, perm2.T.copy(), split, join, fold)]


def part_of(m):
    return 4 * (m % 2) + 2 * (m // 2 % 2) + m // 4


def body(
    ns, nspace,
    *refs,
):
    given, results, inputs, rest = refs[:13], refs[13:16], refs[16:29], refs[29:]
    work(ns, nspace, given, results, inputs, *rest)


def work(
    ns, nspace, given, results, inputs,
    f_land, ff, tt, patches, win, win_t, wdt, wd, wu, wut, bd, bdt, wf, wb, wa,
    act, slope, cots, cot_t, bm, term, red, r_land, bc, b_land, rolled, act_c, pred_t,
    red_out, bc_out,
    gi_wide, gc, e_rest, e_send, e_recv, l_send, l_recv, late, ez_out, ez_all, lz_out, lz_all,
    e_out, e_all, l_out, l_all,
    near_p, near_z, wide_p, wide_z, in_s, halo_ss, halo_rs,
    e_ss, e_rs, l_ss, l_rs, z_ss, z_rs, y_ss, y_rs, a_ss, a_rs, b_ss, b_rs,
):
    fields, cot, w_in, w_dn, w_co, w_up, w_out, perm, perm2, perm2t, split, join, fold = inputs
    pred, got_e, got_l = results
    nzg = nspace // HIGH
    nxy = ns * HIGH
    s = lax.axis_index("sample")
    sp = lax.axis_index("space")
    high, zi = sp // nzg, lax.rem(sp, nzg)
    me = high * ns + s
    left = lax.rem(sp + nspace - 1, nspace)
    right = lax.rem(sp + 1, nspace)
    has_left = jnp.where(sp > 0, 1.0, 0.0).astype(F32)
    has_right = jnp.where(sp < nspace - 1, 1.0, 0.0).astype(F32)

    def plane_peer(i):
        peer = lax.rem(me + i, nxy)
        return peer, (lax.rem(peer, ns), (peer // ns) * nzg + zi)

    def z_peer(i):
        peer = lax.rem(zi + i, nzg)
        return peer, (s, high * nzg + peer)

    barrier = pltpu.get_barrier_semaphore()

    def greet(device):
        pl.semaphore_signal(barrier, inc=1, device_id=device, device_id_type=MESH)

    xs, pair = s // 4, lax.rem(s, 4)
    mates = [xs * 4 + lax.rem(pair + i, 4) for i in (1, 2, 3)]
    ring = [lax.rem(xs + i, ns // 4) * 4 + pair for i in range(1, ns // 4)]

    def along_z(i):
        return (s, high * nzg + lax.rem(zi + i + nzg, nzg))

    opposite = (s, (1 - high) * nzg + zi)
    greeted = [(s, left), (s, right), opposite]
    greeted += [(mate, sp) for mate in mates] + [(other, sp) for other in ring]
    greeted += [along_z(i) for i in (1, -1, 2, -2)]
    for device in greeted:
        greet(device)

    def tell(sem, devices):
        for device in devices:
            pl.semaphore_signal(sem, inc=1, device_id=device, device_id_type=MESH)

    loads = [
        pltpu.make_async_copy(src, dst, in_s.at[i])
        for i, (src, dst) in enumerate(zip(given, inputs))
    ]
    for i in (0, 2, 12, 3, 5, 6, 4, 1, 8, 10, 7, 9, 11):
        loads[i].start()
    loads[0].wait()
    pl.semaphore_wait(barrier, len(greeted))

    def halo(step, to_left, to_right, from_left, from_right):
        copies = [
            pltpu.make_async_remote_copy(
                src_ref=to_right, dst_ref=from_left, send_sem=halo_ss.at[2 * step],
                recv_sem=halo_rs.at[2 * step], device_id=(s, right), device_id_type=MESH,
            ),
            pltpu.make_async_remote_copy(
                src_ref=to_left, dst_ref=from_right, send_sem=halo_ss.at[2 * step + 1],
                recv_sem=halo_rs.at[2 * step + 1], device_id=(s, left), device_id_type=MESH,
            ),
        ]
        for copy in copies:
            copy.start()
        return copies

    def finish(copies):
        for copy in copies:
            copy.wait()

    nf, ny, nz = fields.shape[1], fields.shape[3], fields.shape[4]
    c1, c2 = w_up.shape[1], w_up.shape[2]
    yc = ny // 2
    cells = yc * LANES
    chunks = cells // CHUNK
    fr = 4 * nf
    hr = 2 * nf

    def halo_chunk(step, n, src, land):
        return halo(
            step * chunks + n + 1, src.at[n], src.at[n], land.at[0, n], land.at[1, n]
        )

    f_copies = halo(0, fields.at[0, :, 0], fields.at[0, :, 1], f_land.at[0], f_land.at[1])
    tell(near_p, [(mate, sp) for mate in mates])
    tell(near_z, [along_z(2), along_z(-2)])
    for i in (2, 12, 3, 5, 6, 4):
        loads[i].wait()

    win_t[...] = jnp.zeros_like(win_t)
    for k in range(27):
        win_t[k * nf : (k + 1) * nf, 0:c1] = w_in[k].astype(F32)
    flat = win_t[...].T[0:c1, :].astype(BF)
    spread_w = dot(flat, fold[...]).astype(BF)
    for m in range(8):
        win[m * c1 : (m + 1) * c1, :] = spread_w[:, m * 64 * nf : (m + 1) * 64 * nf]
        wdt[m * c1 : (m + 1) * c1, :] = w_dn[part_of(m)]
        wu[m * c1 : (m + 1) * c1, :] = w_up[part_of(m)]
    wd[...] = wdt[...].astype(F32).T.astype(BF)
    wut[...] = wu[...].astype(F32).T.astype(BF)
    bd[...] = jnp.zeros_like(bd)
    for m in range(8):
        bd[m * nf : (m + 1) * nf, m * c1 : (m + 1) * c1] = w_out[...].astype(F32)
    bdt[...] = bd[...].T.astype(BF)
    bd_b = bd[...].astype(BF)
    for q in range(3):
        for a in range(3):
            wf[q, :, a * c2 : (a + 1) * c2] = jnp.concatenate(
                [w_co[9 * a + 3 * q + b] for b in range(3)], axis=0
            ).astype(F32)
            for b in range(3):
                wa[q, a * c2 : (a + 1) * c2, b * c2 : (b + 1) * c2] = w_co[
                    9 * (2 - a) + 3 * (2 - q) + b
                ].astype(F32)
        wb[q] = wa[q].T.astype(BF)

    for i in (1, 8, 10, 7, 9, 11):
        loads[i].wait()
    cot_rows = cot[0].astype(F32).reshape(2 * nf * ny, nz).astype(BF)
    cot_t[...] = dot(dot(perm2[...], cot_rows).astype(BF), split[:, LANES : 3 * LANES]).astype(BF)
    for y in range(yc):
        for m in range(2):
            cots[m * 2 * hr : (m + 1) * 2 * hr, y * LANES : (y + 1) * LANES] = cot_t[
                y * 2 * hr : (y + 1) * 2 * hr, m * LANES : (m + 1) * LANES
            ]
    for n in range(chunks):
        at = slice(n * CHUNK, (n + 1) * CHUNK)
        back = dot(bdt[...], cots[:, at]).astype(BF)
        bm[:, at] = back
        term[:, at] = dot(wut[...], back)

    rows = nf * ny
    ff[0 : 2 * rows, :] = fields[0].astype(F32).reshape(2 * rows, nz).astype(BF)
    finish(f_copies)
    pl.semaphore_wait(near_p, 3)
    tell(wide_p, [opposite])
    pl.semaphore_wait(near_z, 2)
    tell(wide_z, [along_z(4), along_z(-4)])
    ff[2 * rows : 3 * rows, :] = (f_land[0].astype(F32).reshape(rows, nz) * has_left).astype(BF)
    ff[3 * rows : 4 * rows, :] = (f_land[1].astype(F32).reshape(rows, nz) * has_right).astype(BF)
    tt[...] = dot(dot(perm[...], ff[...]).astype(BF), split[...]).astype(BF)
    for y in range(yc):
        for dy in range(4):
            for dz in range(4):
                patches[(dy * 4 + dz) * fr : (dy * 4 + dz + 1) * fr, y * LANES : (y + 1) * LANES] = tt[
                    (2 * y + dy) * fr : (2 * y + dy + 1) * fr, dz * LANES : (dz + 1) * LANES
                ]
    r_copies = []
    for n in range(chunks):
        at = slice(n * CHUNK, (n + 1) * CHUNK)
        pre = dot(win[...], patches[:, at])
        sigma = jax.nn.sigmoid(pre)
        fine = (pre * sigma).astype(BF)
        slope[:, at] = sigma * (1.0 + pre * (1.0 - sigma))
        act[:, at] = fine
        down = dot(wd[...], fine).astype(BF)
        red_out[n] = down
        red[c2 : 2 * c2, LANES + n * CHUNK : LANES + (n + 1) * CHUNK] = down
        r_copies.append(halo_chunk(0, n, red_out, r_land))
    edge = jnp.zeros((3 * c2, LANES), BF)
    for planes in (red, bc):
        planes[:, 0:LANES] = edge
        planes[:, LANES + cells : 2 * LANES + cells] = edge

    def arrive(n, copies, land, planes):
        finish(copies[n])
        there = slice(LANES + n * CHUNK, LANES + (n + 1) * CHUNK)
        planes[0:c2, there] = (land[0, n].astype(F32) * has_left).astype(BF)
        planes[2 * c2 : 3 * c2, there] = (land[1, n].astype(F32) * has_right).astype(BF)


    lane = lax.rem(lax.broadcasted_iota(jnp.int32, (c2, CHUNK), 1), LANES)
    not_first, not_last = lane > 0, lane < LANES - 1

    def later(v):
        return jnp.where(not_first, pltpu.roll(v, 1, 1), 0.0)

    def sooner(v):
        return jnp.where(not_last, pltpu.roll(v, CHUNK - 1, 1), 0.0)

    wf_b = [wf[q].astype(BF) for q in range(3)]

    b_copies = []
    arrive(0, r_copies, r_land, red)
    for n in range(chunks):
        if n + 1 < chunks:
            arrive(n + 1, r_copies, r_land, red)
        at = slice(n * CHUNK, (n + 1) * CHUNK)
        out = sum(
            dot(wf_b[q], red[:, n * CHUNK + q * LANES : (n + 1) * CHUNK + q * LANES])
            for q in range(3)
        )
        pre = out[c2 : 2 * c2] + later(out[0:c2]) + sooner(out[2 * c2 : 3 * c2])
        sigma = jax.nn.sigmoid(pre)
        act_c[:, at] = (pre * sigma).astype(BF)
        back = (term[:, at] * (sigma * (1.0 + pre * (1.0 - sigma)))).astype(BF)
        bc_out[n] = back
        bc[c2 : 2 * c2, LANES + n * CHUNK : LANES + (n + 1) * CHUNK] = back
        b_copies.append(halo_chunk(1, n, bc_out, b_land))
        wide = back.astype(F32)
        rolled[0:c2, at] = sooner(wide).astype(BF)
        rolled[c2 : 2 * c2, at] = back
        rolled[2 * c2 : 3 * c2, at] = later(wide).astype(BF)

    for q in range(3):
        gc[q * 3 * c2 : (q + 1) * 3 * c2, :] = dot_nt(
            rolled[...], red[:, q * LANES : q * LANES + cells]
        )
    def plane_copy(i, src, dst, send_sem, recv_sem):
        return pltpu.make_async_remote_copy(
            src_ref=src, dst_ref=dst, send_sem=send_sem, recv_sem=recv_sem,
            device_id=plane_peer(i)[1], device_id_type=MESH,
        )

    def send_early(h):
        def one(i, carry):
            plane_copy(
                i, e_send.at[h, plane_peer(i)[0]], e_recv.at[h, i], e_ss.at[h], e_rs.at[h]
            ).start()
            return carry

        lax.fori_loop(1, nxy, one, 0)
        e_recv[h, 0] = e_send[h, me]

    e_rows = e_send.shape[2]
    head = nxy * e_rows
    pl.semaphore_wait(wide_p, 1)
    pl.semaphore_wait(wide_z, 2)
    e_send[0] = gc[0:head, 0:LANES].astype(BF).reshape(nxy, e_rows, LANES)
    send_early(0)

    g_out_wide = jnp.zeros((8 * nf, 8 * c1), F32)
    for n in range(chunks):
        at = slice(n * CHUNK, (n + 1) * CHUNK)
        merged = (act[:, at].astype(F32) + dot(wu[...], act_c[:, at])).astype(BF)
        out = dot(bd_b, merged).astype(BF)
        g_out_wide = g_out_wide + dot_nt(cots[:, at], merged)
        for y in range(CHUNK // LANES):
            for m in range(2):
                pred_t[
                    (n * (CHUNK // LANES) + y) * 2 * hr : (n * (CHUNK // LANES) + y + 1) * 2 * hr,
                    m * LANES : (m + 1) * LANES,
                ] = out[m * 2 * hr : (m + 1) * 2 * hr, y * LANES : (y + 1) * LANES]
    gu = dot_nt(bm[...], act_c[...])
    mine = (
        lax.broadcasted_iota(jnp.int32, (8 * nf, 8 * c1), 0) // nf
        == lax.broadcasted_iota(jnp.int32, (8 * nf, 8 * c1), 1) // c1
    )
    g_out_wide = jnp.where(mine, g_out_wide, 0.0)
    g_out_half = g_out_wide[:, 0:LANES] + g_out_wide[:, LANES : 2 * LANES]
    g_out_half = g_out_half + pltpu.roll(g_out_half, 64, 1)
    g_out_half = g_out_half + pltpu.roll(g_out_half, 32, 1)
    g_out_half = g_out_half[0:8] + g_out_half[8:16] + g_out_half[16:24] + g_out_half[24:32]
    g_out_half = g_out_half + pltpu.roll(g_out_half, 4, 0)

    half = 9 * c2 // 2
    tail = 9 * c2 - head
    e_rest[0:tail, :] = gc[head:, 0:LANES].astype(BF)
    e_rest[tail : tail + half, 0:c2] = gc[0:half, LANES : LANES + c2].astype(BF)
    e_rest[tail : tail + half, c2 : 2 * c2] = gc[half : 2 * half, LANES : LANES + c2].astype(BF)
    up_at = tail + half
    e_rest[up_at : up_at + LANES, 0:c2] = gu[0:LANES].astype(BF)
    e_rest[up_at : up_at + LANES, c2 : 2 * c2] = gu[LANES : 2 * LANES].astype(BF)
    out_at = up_at + LANES
    e_rest[out_at : out_at + 32, :] = jnp.concatenate(
        [g_out_half, jnp.zeros((24, LANES), F32)], axis=0
    ).astype(BF)
    e_send[1] = e_rest[...].reshape(nxy, e_rows, LANES)
    send_early(1)

    arrive(0, b_copies, b_land, bc)
    gd = jnp.zeros((8 * c1, c2), F32)
    gi = jnp.zeros((8 * c1, 64 * nf), F32)
    for n in range(chunks):
        if n + 1 < chunks:
            arrive(n + 1, b_copies, b_land, bc)
        at = slice(n * CHUNK, (n + 1) * CHUNK)
        out = sum(
            dot(wb[q], bc[:, n * CHUNK + q * LANES : (n + 1) * CHUNK + q * LANES])
            for q in range(3)
        )
        back = out[c2 : 2 * c2] + sooner(out[0:c2]) + later(out[2 * c2 : 3 * c2])
        back = back.astype(BF)
        fine = ((bm[:, at].astype(F32) + dot(wdt[...], back)) * slope[:, at]).astype(BF)
        gd = gd + dot_nt(act[:, at], back)
        gi = gi + dot_nt(fine, patches[:, at])
    late[0:LANES, 0:c2] = gd[0:LANES]
    late[0:LANES, c2 : 2 * c2] = gd[LANES : 2 * LANES]
    gi = gi.astype(BF)
    for m in range(8):
        gi_wide[:, m * 64 * nf : (m + 1) * 64 * nf] = gi[m * c1 : (m + 1) * c1, :]
    late[LANES : LANES + c1, :] = dot_nt(gi_wide[...], fold[...])
    l_rows = (LANES + c1) // nxy
    for p in range(nxy):
        l_send[p, 0:l_rows, :] = late[p * l_rows : (p + 1) * l_rows, :]

    def send_late(i, carry):
        plane_copy(i, l_send.at[plane_peer(i)[0], 0:l_rows], l_recv.at[i, 0:l_rows], l_ss, l_rs).start()
        return carry

    lax.fori_loop(1, nxy, send_late, 0)
    l_recv[0, 0:l_rows, :] = l_send[me, 0:l_rows, :]

    def all_of(ref, sem, count, rows=None):
        block = ref.at[pl.ds(0, count)] if rows is None else ref.at[pl.ds(0, count), 0:rows]
        pltpu.make_async_copy(block, block, sem).wait()

    def send_z(src, dst, send_sem, recv_sem):
        def one(i):
            pltpu.make_async_remote_copy(
                src_ref=src, dst_ref=dst, send_sem=send_sem, recv_sem=recv_sem,
                device_id=z_peer(i)[1], device_id_type=MESH,
            ).start()

        def both(i, carry):
            one(nzg // 2 + i)
            one(nzg // 2 - i)
            return carry

        one(nzg // 2)
        lax.fori_loop(1, nzg // 2, both, 0)

    def send_plane(src, dst, send_sem, recv_sem):
        def one(i, carry):
            plane_copy(i, src, dst, send_sem, recv_sem).start()
            return carry

        lax.fori_loop(1, nxy, one, 0)

    def early_z(h):
        all_of(e_recv.at[h], e_rs.at[h], nxy - 1)
        part = jnp.sum(e_recv[h].astype(F32), axis=0).astype(BF)
        ez_out[h] = part
        ez_all[h, zi] = part
        send_z(ez_out.at[h], ez_all.at[h, zi], z_ss.at[h], z_rs.at[h])

    def early_back(h):
        all_of(ez_all.at[h], z_rs.at[h], nzg - 1)
        part = jnp.sum(ez_all[h].astype(F32), axis=0).astype(BF)
        e_out[h] = part
        e_all[h, me] = part
        send_plane(e_out.at[h], e_all.at[h, me], a_ss.at[h], a_rs.at[h])

    early_z(0)
    early_z(1)

    out = dot(dot(perm2t[...], pred_t[...]).astype(BF), join[...])
    pred[0] = out.reshape(nf, 2, ny, nz).astype(BF)

    all_of(l_recv, l_rs, nxy - 1, l_rows)
    part = jnp.sum(l_recv[:, 0:l_rows, :], axis=0)
    lz_out[0:l_rows, :] = part
    lz_all[zi, 0:l_rows, :] = part
    send_z(lz_out.at[0:l_rows], lz_all.at[zi, 0:l_rows], y_ss, y_rs)

    early_back(0)
    early_back(1)

    all_of(lz_all, y_rs, nzg - 1, l_rows)
    part = jnp.sum(lz_all[:, 0:l_rows, :], axis=0)
    l_out[0:l_rows, :] = part
    l_all[me, 0:l_rows, :] = part
    send_plane(l_out.at[0:l_rows], l_all.at[me, 0:l_rows], b_ss, b_rs)

    all_of(l_send, l_ss, nxy - 1, l_rows)
    all_of(lz_all, y_ss, nzg - 1, l_rows)
    for h in range(2):
        all_of(e_send.at[h], e_ss.at[h], nxy - 1)
        all_of(ez_all.at[h], z_ss.at[h], nzg - 1)
        all_of(e_all.at[h], a_rs.at[h], nxy - 1)
    got_e[...] = e_all[...]
    all_of(l_all, b_rs, nxy - 1, l_rows)
    got_l[...] = l_all[...]
    for h in range(2):
        all_of(e_all.at[h], a_ss.at[h], nxy - 1)
    all_of(l_all, b_ss, nxy - 1, l_rows)


def leave(
    prediction, got_e, got_l, pred, g_in, g_dn, g_co, g_up, g_out, full, late, win_t
):
    nf, c1 = g_out.shape
    c2 = g_co.shape[1]
    nxy, e_rows = got_e.shape[1], got_e.shape[2]
    l_rows = (LANES + c1) // nxy
    head, half = nxy * e_rows, 9 * c2 // 2
    pred[...] = prediction[...]
    win_t[...] = jnp.zeros_like(win_t)
    full[0:head, :] = got_e[0].astype(F32).reshape(head, LANES)
    full[head : 2 * head, :] = got_e[1].astype(F32).reshape(head, LANES)
    for n in range(9):
        block = full[n * c2 : (n + 1) * c2, :]
        g_co[n] = block[:, 0:c2]
        g_co[9 + n] = pltpu.roll(block, c2, 1)[:, 0:c2]
    for n in range(9):
        row = 9 * c2 + (n * c2) % half
        lo = min(c2, half - (n * c2) % half)
        block = full[row : row + lo, :]
        if n * c2 // half == 1:
            block = pltpu.roll(block, c2, 1)
        g_co[18 + n, 0:lo, :] = block[:, 0:c2]
        if lo < c2:
            rest = pltpu.roll(full[9 * c2 : 9 * c2 + c2 - lo, :], c2, 1)
            g_co[18 + n, lo:c2, :] = rest[:, 0:c2]
    up_at = 9 * c2 + half
    out_at = up_at + LANES
    for m in range(4):
        block = full[up_at + m * c1 : up_at + (m + 1) * c1, :]
        g_up[part_of(m)] = block[:, 0:c2]
        g_up[part_of(m + 4)] = pltpu.roll(block, c2, 1)[:, 0:c2]
    g_out[...] = full[out_at : out_at + nf, 0:c1]
    for p in range(nxy):
        late[p * l_rows : (p + 1) * l_rows, :] = got_l[p, 0:l_rows, :]
    for m in range(4):
        block = late[m * c1 : (m + 1) * c1, :]
        g_dn[part_of(m)] = block[:, 0:c2]
        g_dn[part_of(m + 4)] = pltpu.roll(block, c2, 1)[:, 0:c2]
    win_t[0:c1, :] = late[LANES : LANES + c1, :]
    flipped = win_t[...].T
    for k in range(27):
        g_in[k] = flipped[k * nf : (k + 1) * nf, 0:c1]


def shards(fields, cotangent, w_in, w_down, w_coarse, w_up, w_out):
    ns, nspace = lax.axis_size("sample"), lax.axis_size("space")
    nf, ny, nz = fields.shape[1], fields.shape[3], fields.shape[4]
    c1, c2 = w_up.shape[1], w_up.shape[2]
    cells = (ny // 2) * (nz // 2)
    nxy, nzg = ns * HIGH, nspace // HIGH
    e_rows = (9 * c2 * 3 // 2 + LANES + 32) // (2 * nxy)
    l_rows = (LANES + c1) // nxy
    lr = -(-l_rows // 8) * 8
    wide = 64 * nf
    consts = one_hots(ny, nz, nf)
    vm = pltpu.VMEM
    dma = pltpu.SemaphoreType.DMA
    regular = pltpu.SemaphoreType.REGULAR
    given = (
        fields, cotangent, w_in.transpose(0, 2, 1), w_down.transpose(0, 2, 1), w_coarse, w_up,
        w_out, *consts,
    )
    scratch = [vm(v.shape, v.dtype) for v in given] + [
        vm((2, nf, ny, nz), BF),
        vm((4 * nf * ny, nz), BF),
        vm(((ny + 2) * 4 * nf, 4 * LANES), BF),
        vm((wide, cells), BF),
        vm((8 * c1, wide), BF),
        vm((128, 128), F32),
        vm((8 * c1, c2), BF),
        vm((c2, 8 * c1), BF),
        vm((8 * c1, c2), BF),
        vm((c2, 8 * c1), BF),
        vm((8 * nf, 8 * c1), F32),
        vm((8 * c1, 8 * nf), BF),
        vm((3, 3 * c2, 3 * c2), F32),
        vm((3, 3 * c2, 3 * c2), BF),
        vm((3, 3 * c2, 3 * c2), F32),
        vm((8 * c1, cells), BF),
        vm((8 * c1, cells), F32),
        vm((8 * nf, cells), BF),
        vm((2 * nf * ny, 2 * LANES), BF),
        vm((8 * c1, cells), BF),
        vm((c2, cells), F32),
        vm((3 * c2, cells + 2 * LANES), BF),
        vm((2, cells // CHUNK, c2, CHUNK), BF),
        vm((3 * c2, cells + 2 * LANES), BF),
        vm((2, cells // CHUNK, c2, CHUNK), BF),
        vm((3 * c2, cells), BF),
        vm((c2, cells), BF),
        vm((2 * nf * ny, 2 * LANES), BF),
        vm((cells // CHUNK, c2, CHUNK), BF),
        vm((cells // CHUNK, c2, CHUNK), BF),
        vm((c1, 8 * wide), BF),
        vm((9 * c2, 3 * c2), F32),
        vm((nxy * e_rows, LANES), BF),
        vm((2, nxy, e_rows, LANES), BF),
        vm((2, nxy, e_rows, LANES), BF),
        vm((nxy, lr, LANES), F32),
        vm((nxy, lr, LANES), F32),
        vm((LANES + c1, LANES), F32),
        vm((2, e_rows, LANES), BF),
        vm((2, nzg, e_rows, LANES), BF),
        vm((lr, LANES), F32),
        vm((nzg, lr, LANES), F32),
        vm((2, e_rows, LANES), BF),
        vm((2, nxy, e_rows, LANES), BF),
        vm((lr, LANES), F32),
        vm((nxy, lr, LANES), F32),
        regular, regular, regular, regular, dma((13,)), dma((2 + 4 * cells // CHUNK,)), dma((2 + 4 * cells // CHUNK,)),
        dma((2,)), dma((2,)), dma, dma, dma((2,)), dma((2,)), dma, dma, dma((2,)), dma((2,)), dma, dma,
    ]
    shape = jax.ShapeDtypeStruct
    whole = pl.BlockSpec(memory_space=pltpu.VMEM)
    far = pl.BlockSpec(memory_space=pltpu.HBM)
    shapes = (
        shape(fields.shape, BF),
        shape((27, nf, c1), F32),
        shape((8, c1, c2), F32),
        shape((27, c2, c2), F32),
        shape((8, c1, c2), F32),
        shape((nf, c1), F32),
    )
    outs = pl.pallas_call(
        functools.partial(body, ns, nspace),
        out_shape=(
            shapes[0], shape((2, nxy, e_rows, LANES), BF), shape((nxy, lr, LANES), F32),
        ),
        in_specs=[far] * 13,
        out_specs=[whole] * 3,
        scratch_shapes=scratch,
        compiler_params=pltpu.CompilerParams(
            collective_id=0, has_side_effects=True, vmem_limit_bytes=VMEM
        ),
        name="unet_block",
    )(*given)
    outs = pl.pallas_call(
        leave,
        out_shape=shapes,
        in_specs=[whole] * 3,
        out_specs=[whole] * 6,
        scratch_shapes=[
            vm((2 * nxy * e_rows, LANES), F32), vm((LANES + c1, LANES), F32), vm((128, 128), F32),
        ],
        compiler_params=pltpu.CompilerParams(vmem_limit_bytes=VMEM),
        name="leave",
    )(*outs)
    prediction, g_in, g_dn, g_co, g_up, g_out = outs
    return (prediction, g_in.transpose(0, 2, 1), g_dn.transpose(0, 2, 1), g_co, g_up, g_out)


def solution(mesh):
    split = P("sample", None, "space", None, None)
    return jax.shard_map(
        shards,
        mesh=mesh,
        in_specs=(split, split, P(), P(), P(), P(), P()),
        out_specs=(split, P(), P(), P(), P(), P()),
        check_vma=False,
    )
```

```python
import functools

import jax
import jax.numpy as jnp
import numpy as np
from jax import lax
from jax.experimental import pallas as pl
from jax.experimental.pallas import tpu as pltpu
from jax.sharding import PartitionSpec as P

MESH = pl.DeviceIdType.MESH
BF = jnp.bfloat16
F32 = jnp.float32
LANES = 128
CHUNK = 512
VMEM = 63 * 2**20
HIGH = 2


def dot(a, b):
    return lax.dot_general(a, b, (((1,), (0,)), ((), ())), preferred_element_type=F32)


def dot_nt(a, b):
    return lax.dot_general(a, b, (((1,), (1,)), ((), ())), preferred_element_type=F32)


def one_hots(ny, nz, nf):
    wide = nz // 2
    rows = (ny + 2) * 4 * nf
    perm = np.zeros((rows, 4 * nf * ny), np.float32)
    own = 2 * nf * ny
    for y in range(ny):
        for f in range(nf):
            for dx in range(4):
                if dx == 0:
                    source = own + f * ny + y
                elif dx == 3:
                    source = own + nf * ny + f * ny + y
                else:
                    source = (f * 2 + dx - 1) * ny + y
                perm[(y + 1) * 4 * nf + dx * nf + f, source] = 1
    perm2 = np.zeros((2 * nf * ny, 2 * nf * ny), np.float32)
    for y in range(ny):
        for x in range(2):
            for f in range(nf):
                perm2[y * 2 * nf + x * nf + f, (f * 2 + x) * ny + y] = 1
    split = np.zeros((nz, 4 * wide), np.float32)
    for d in range(4):
        for z in range(wide):
            if 0 <= 2 * z + d - 1 < nz:
                split[2 * z + d - 1, d * wide + z] = 1
    join = split[:, wide : 3 * wide].T.copy()
    fold = np.zeros((128, 8 * 64 * nf), np.float32)
    for m in range(8):
        mz, my, mx = m // 4, m // 2 % 2, m % 2
        for k in range(27):
            dx, dy, dz = k // 9 + mx, k // 3 % 3 + my, k % 3 + mz
            for c in range(nf):
                fold[k * nf + c, m * 64 * nf + (dy * 4 + dz) * 4 * nf + dx * nf + c] = 1
    return [jnp.asarray(v, BF) for v in (perm, perm2, perm2.T.copy(), split, join, fold)]


def part_of(m):
    return 4 * (m % 2) + 2 * (m // 2 % 2) + m // 4


def body(
    ns, nspace,
    *refs,
):
    given, results, inputs, rest = refs[:13], refs[13:16], refs[16:29], refs[29:]
    work(ns, nspace, given, results, inputs, *rest)


def work(
    ns, nspace, given, results, inputs,
    f_land, ff, tt, patches, win, win_t, wdt, wd, wu, wut, bd, bdt, wf, wb, wa,
    act, slope, cots, cot_t, bm, term, red, r_land, bc, b_land, rolled, act_c, pred_t,
    red_out, bc_out,
    gi_wide, gc, e_rest, e_send, e_recv, l_send, l_recv, late, ez_out, ez_all, lz_out, lz_all,
    e_out, e_all, l_out, l_all,
    near_p, near_z, wide_p, wide_z, in_s, halo_ss, halo_rs,
    e_ss, e_rs, l_ss, l_rs, z_ss, z_rs, y_ss, y_rs, a_ss, a_rs, b_ss, b_rs,
):
    fields, cot, w_in, w_dn, w_co, w_up, w_out, perm, perm2, perm2t, split, join, fold = inputs
    pred, got_e, got_l = results
    nzg = nspace // HIGH
    nxy = ns * HIGH
    s = lax.axis_index("sample")
    sp = lax.axis_index("space")
    high, zi = sp // nzg, lax.rem(sp, nzg)
    me = high * ns + s
    left = lax.rem(sp + nspace - 1, nspace)
    right = lax.rem(sp + 1, nspace)
    has_left = jnp.where(sp > 0, 1.0, 0.0).astype(F32)
    has_right = jnp.where(sp < nspace - 1, 1.0, 0.0).astype(F32)

    def plane_peer(i):
        peer = lax.rem(me + i, nxy)
        return peer, (lax.rem(peer, ns), (peer // ns) * nzg + zi)

    def z_peer(i):
        peer = lax.rem(zi + i, nzg)
        return peer, (s, high * nzg + peer)

    barrier = pltpu.get_barrier_semaphore()

    def greet(device):
        pl.semaphore_signal(barrier, inc=1, device_id=device, device_id_type=MESH)

    xs, pair = s // 4, lax.rem(s, 4)
    mates = [xs * 4 + lax.rem(pair + i, 4) for i in (1, 2, 3)]
    ring = [lax.rem(xs + i, ns // 4) * 4 + pair for i in range(1, ns // 4)]

    def along_z(i):
        return (s, high * nzg + lax.rem(zi + i + nzg, nzg))

    opposite = (s, (1 - high) * nzg + zi)
    greeted = [(s, left), (s, right), opposite]
    greeted += [(mate, sp) for mate in mates] + [(other, sp) for other in ring]
    greeted += [along_z(i) for i in (1, -1, 2, -2)]
    for device in greeted:
        greet(device)

    def tell(sem, devices):
        for device in devices:
            pl.semaphore_signal(sem, inc=1, device_id=device, device_id_type=MESH)

    loads = [
        pltpu.make_async_copy(src, dst, in_s.at[i])
        for i, (src, dst) in enumerate(zip(given, inputs))
    ]
    for i in (0, 2, 12, 3, 5, 6, 4, 1, 8, 10, 7, 9, 11):
        loads[i].start()
    loads[0].wait()
    pl.semaphore_wait(barrier, len(greeted))

    def halo(step, to_left, to_right, from_left, from_right):
        copies = [
            pltpu.make_async_remote_copy(
                src_ref=to_right, dst_ref=from_left, send_sem=halo_ss.at[2 * step],
                recv_sem=halo_rs.at[2 * step], device_id=(s, right), device_id_type=MESH,
            ),
            pltpu.make_async_remote_copy(
                src_ref=to_left, dst_ref=from_right, send_sem=halo_ss.at[2 * step + 1],
                recv_sem=halo_rs.at[2 * step + 1], device_id=(s, left), device_id_type=MESH,
            ),
        ]
        for copy in copies:
            copy.start()
        return copies

    def finish(copies):
        for copy in copies:
            copy.wait()

    nf, ny, nz = fields.shape[1], fields.shape[3], fields.shape[4]
    c1, c2 = w_up.shape[1], w_up.shape[2]
    yc = ny // 2
    cells = yc * LANES
    chunks = cells // CHUNK
    fr = 4 * nf
    hr = 2 * nf

    def halo_chunk(step, n, src, land):
        return halo(
            step * chunks + n + 1, src.at[n], src.at[n], land.at[0, n], land.at[1, n]
        )

    f_copies = halo(0, fields.at[0, :, 0], fields.at[0, :, 1], f_land.at[0], f_land.at[1])
    tell(near_p, [(mate, sp) for mate in mates])
    tell(near_z, [along_z(2), along_z(-2)])
    for i in (2, 12, 3, 5, 6, 4):
        loads[i].wait()

    win_t[...] = jnp.zeros_like(win_t)
    for k in range(27):
        win_t[k * nf : (k + 1) * nf, 0:c1] = w_in[k].astype(F32)
    flat = win_t[...].T[0:c1, :].astype(BF)
    spread_w = dot(flat, fold[...]).astype(BF)
    for m in range(8):
        win[m * c1 : (m + 1) * c1, :] = spread_w[:, m * 64 * nf : (m + 1) * 64 * nf]
        wdt[m * c1 : (m + 1) * c1, :] = w_dn[part_of(m)]
        wu[m * c1 : (m + 1) * c1, :] = w_up[part_of(m)]
    wd[...] = wdt[...].astype(F32).T.astype(BF)
    wut[...] = wu[...].astype(F32).T.astype(BF)
    bd[...] = jnp.zeros_like(bd)
    for m in range(8):
        bd[m * nf : (m + 1) * nf, m * c1 : (m + 1) * c1] = w_out[...].astype(F32)
    bdt[...] = bd[...].T.astype(BF)
    bd_b = bd[...].astype(BF)
    for q in range(3):
        for a in range(3):
            wf[q, :, a * c2 : (a + 1) * c2] = jnp.concatenate(
                [w_co[9 * a + 3 * q + b] for b in range(3)], axis=0
            ).astype(F32)
            for b in range(3):
                wa[q, a * c2 : (a + 1) * c2, b * c2 : (b + 1) * c2] = w_co[
                    9 * (2 - a) + 3 * (2 - q) + b
                ].astype(F32)
        wb[q] = wa[q].T.astype(BF)

    for i in (1, 8, 10, 7, 9, 11):
        loads[i].wait()
    cot_rows = cot[0].astype(F32).reshape(2 * nf * ny, nz).astype(BF)
    cot_t[...] = dot(dot(perm2[...], cot_rows).astype(BF), split[:, LANES : 3 * LANES]).astype(BF)
    for y in range(yc):
        for m in range(2):
            cots[m * 2 * hr : (m + 1) * 2 * hr, y * LANES : (y + 1) * LANES] = cot_t[
                y * 2 * hr : (y + 1) * 2 * hr, m * LANES : (m + 1) * LANES
            ]
    for n in range(chunks):
        at = slice(n * CHUNK, (n + 1) * CHUNK)
        back = dot(bdt[...], cots[:, at]).astype(BF)
        bm[:, at] = back
        term[:, at] = dot(wut[...], back)

    rows = nf * ny
    ff[0 : 2 * rows, :] = fields[0].astype(F32).reshape(2 * rows, nz).astype(BF)
    finish(f_copies)
    pl.semaphore_wait(near_p, 3)
    tell(wide_p, [opposite])
    pl.semaphore_wait(near_z, 2)
    tell(wide_z, [along_z(4), along_z(-4)])
    ff[2 * rows : 3 * rows, :] = (f_land[0].astype(F32).reshape(rows, nz) * has_left).astype(BF)
    ff[3 * rows : 4 * rows, :] = (f_land[1].astype(F32).reshape(rows, nz) * has_right).astype(BF)
    tt[...] = dot(dot(perm[...], ff[...]).astype(BF), split[...]).astype(BF)
    for y in range(yc):
        for dy in range(4):
            for dz in range(4):
                patches[(dy * 4 + dz) * fr : (dy * 4 + dz + 1) * fr, y * LANES : (y + 1) * LANES] = tt[
                    (2 * y + dy) * fr : (2 * y + dy + 1) * fr, dz * LANES : (dz + 1) * LANES
                ]
    r_copies = []
    for n in range(chunks):
        at = slice(n * CHUNK, (n + 1) * CHUNK)
        pre = dot(win[...], patches[:, at])
        sigma = jax.nn.sigmoid(pre)
        fine = (pre * sigma).astype(BF)
        slope[:, at] = sigma * (1.0 + pre * (1.0 - sigma))
        act[:, at] = fine
        down = dot(wd[...], fine).astype(BF)
        red_out[n] = down
        red[c2 : 2 * c2, LANES + n * CHUNK : LANES + (n + 1) * CHUNK] = down
        r_copies.append(halo_chunk(0, n, red_out, r_land))
    edge = jnp.zeros((3 * c2, LANES), BF)
    for planes in (red, bc):
        planes[:, 0:LANES] = edge
        planes[:, LANES + cells : 2 * LANES + cells] = edge

    def arrive(n, copies, land, planes):
        finish(copies[n])
        there = slice(LANES + n * CHUNK, LANES + (n + 1) * CHUNK)
        planes[0:c2, there] = (land[0, n].astype(F32) * has_left).astype(BF)
        planes[2 * c2 : 3 * c2, there] = (land[1, n].astype(F32) * has_right).astype(BF)


    lane = lax.rem(lax.broadcasted_iota(jnp.int32, (c2, CHUNK), 1), LANES)
    not_first, not_last = lane > 0, lane < LANES - 1

    def later(v):
        return jnp.where(not_first, pltpu.roll(v, 1, 1), 0.0)

    def sooner(v):
        return jnp.where(not_last, pltpu.roll(v, CHUNK - 1, 1), 0.0)

    wf_b = [wf[q].astype(BF) for q in range(3)]

    b_copies = []
    arrive(0, r_copies, r_land, red)
    for n in range(chunks):
        if n + 1 < chunks:
            arrive(n + 1, r_copies, r_land, red)
        at = slice(n * CHUNK, (n + 1) * CHUNK)
        out = sum(
            dot(wf_b[q], red[:, n * CHUNK + q * LANES : (n + 1) * CHUNK + q * LANES])
            for q in range(3)
        )
        pre = out[c2 : 2 * c2] + later(out[0:c2]) + sooner(out[2 * c2 : 3 * c2])
        sigma = jax.nn.sigmoid(pre)
        act_c[:, at] = (pre * sigma).astype(BF)
        back = (term[:, at] * (sigma * (1.0 + pre * (1.0 - sigma)))).astype(BF)
        bc_out[n] = back
        bc[c2 : 2 * c2, LANES + n * CHUNK : LANES + (n + 1) * CHUNK] = back
        b_copies.append(halo_chunk(1, n, bc_out, b_land))
        wide = back.astype(F32)
        rolled[0:c2, at] = sooner(wide).astype(BF)
        rolled[c2 : 2 * c2, at] = back
        rolled[2 * c2 : 3 * c2, at] = later(wide).astype(BF)

    for q in range(3):
        gc[q * 3 * c2 : (q + 1) * 3 * c2, :] = dot_nt(
            rolled[...], red[:, q * LANES : q * LANES + cells]
        )
    def plane_copy(i, src, dst, send_sem, recv_sem):
        return pltpu.make_async_remote_copy(
            src_ref=src, dst_ref=dst, send_sem=send_sem, recv_sem=recv_sem,
            device_id=plane_peer(i)[1], device_id_type=MESH,
        )

    def send_early(h):
        def one(i, carry):
            plane_copy(
                i, e_send.at[h, plane_peer(i)[0]], e_recv.at[h, i], e_ss.at[h], e_rs.at[h]
            ).start()
            return carry

        lax.fori_loop(1, nxy, one, 0)
        e_recv[h, 0] = e_send[h, me]

    e_rows = e_send.shape[2]
    head = nxy * e_rows
    pl.semaphore_wait(wide_p, 1)
    pl.semaphore_wait(wide_z, 2)
    e_send[0] = gc[0:head, 0:LANES].astype(BF).reshape(nxy, e_rows, LANES)
    send_early(0)

    g_out_wide = jnp.zeros((8 * nf, 8 * c1), F32)
    for n in range(chunks):
        at = slice(n * CHUNK, (n + 1) * CHUNK)
        merged = (act[:, at].astype(F32) + dot(wu[...], act_c[:, at])).astype(BF)
        out = dot(bd_b, merged).astype(BF)
        g_out_wide = g_out_wide + dot_nt(cots[:, at], merged)
        for y in range(CHUNK // LANES):
            for m in range(2):
                pred_t[
                    (n * (CHUNK // LANES) + y) * 2 * hr : (n * (CHUNK // LANES) + y + 1) * 2 * hr,
                    m * LANES : (m + 1) * LANES,
                ] = out[m * 2 * hr : (m + 1) * 2 * hr, y * LANES : (y + 1) * LANES]
    gu = dot_nt(bm[...], act_c[...])
    mine = (
        lax.broadcasted_iota(jnp.int32, (8 * nf, 8 * c1), 0) // nf
        == lax.broadcasted_iota(jnp.int32, (8 * nf, 8 * c1), 1) // c1
    )
    g_out_wide = jnp.where(mine, g_out_wide, 0.0)
    g_out_half = g_out_wide[:, 0:LANES] + g_out_wide[:, LANES : 2 * LANES]
    g_out_half = g_out_half + pltpu.roll(g_out_half, 64, 1)
    g_out_half = g_out_half + pltpu.roll(g_out_half, 32, 1)
    g_out_half = g_out_half[0:8] + g_out_half[8:16] + g_out_half[16:24] + g_out_half[24:32]
    g_out_half = g_out_half + pltpu.roll(g_out_half, 4, 0)

    half = 9 * c2 // 2
    tail = 9 * c2 - head
    e_rest[0:tail, :] = gc[head:, 0:LANES].astype(BF)
    e_rest[tail : tail + half, 0:c2] = gc[0:half, LANES : LANES + c2].astype(BF)
    e_rest[tail : tail + half, c2 : 2 * c2] = gc[half : 2 * half, LANES : LANES + c2].astype(BF)
    up_at = tail + half
    e_rest[up_at : up_at + LANES, 0:c2] = gu[0:LANES].astype(BF)
    e_rest[up_at : up_at + LANES, c2 : 2 * c2] = gu[LANES : 2 * LANES].astype(BF)
    out_at = up_at + LANES
    e_rest[out_at : out_at + 32, :] = jnp.concatenate(
        [g_out_half, jnp.zeros((24, LANES), F32)], axis=0
    ).astype(BF)
    e_send[1] = e_rest[...].reshape(nxy, e_rows, LANES)
    send_early(1)

    arrive(0, b_copies, b_land, bc)
    gd = jnp.zeros((8 * c1, c2), F32)
    gi = jnp.zeros((8 * c1, 64 * nf), F32)
    for n in range(chunks):
        if n + 1 < chunks:
            arrive(n + 1, b_copies, b_land, bc)
        at = slice(n * CHUNK, (n + 1) * CHUNK)
        out = sum(
            dot(wb[q], bc[:, n * CHUNK + q * LANES : (n + 1) * CHUNK + q * LANES])
            for q in range(3)
        )
        back = out[c2 : 2 * c2] + sooner(out[0:c2]) + later(out[2 * c2 : 3 * c2])
        back = back.astype(BF)
        fine = ((bm[:, at].astype(F32) + dot(wdt[...], back)) * slope[:, at]).astype(BF)
        gd = gd + dot_nt(act[:, at], back)
        gi = gi + dot_nt(fine, patches[:, at])
    late[0:LANES, 0:c2] = gd[0:LANES]
    late[0:LANES, c2 : 2 * c2] = gd[LANES : 2 * LANES]
    gi = gi.astype(BF)
    for m in range(8):
        gi_wide[:, m * 64 * nf : (m + 1) * 64 * nf] = gi[m * c1 : (m + 1) * c1, :]
    late[LANES : LANES + c1, :] = dot_nt(gi_wide[...], fold[...])
    l_rows = (LANES + c1) // nxy
    for p in range(nxy):
        l_send[p, 0:l_rows, :] = late[p * l_rows : (p + 1) * l_rows, :]

    def send_late(i, carry):
        plane_copy(i, l_send.at[plane_peer(i)[0], 0:l_rows], l_recv.at[i, 0:l_rows], l_ss, l_rs).start()
        return carry

    lax.fori_loop(1, nxy, send_late, 0)
    l_recv[0, 0:l_rows, :] = l_send[me, 0:l_rows, :]

    def all_of(ref, sem, count, rows=None):
        block = ref.at[pl.ds(0, count)] if rows is None else ref.at[pl.ds(0, count), 0:rows]
        pltpu.make_async_copy(block, block, sem).wait()

    def send_z(src, dst, send_sem, recv_sem):
        def one(i):
            pltpu.make_async_remote_copy(
                src_ref=src, dst_ref=dst, send_sem=send_sem, recv_sem=recv_sem,
                device_id=z_peer(i)[1], device_id_type=MESH,
            ).start()

        def both(i, carry):
            one(nzg // 2 + i)
            one(nzg // 2 - i)
            return carry

        one(nzg // 2)
        lax.fori_loop(1, nzg // 2, both, 0)

    def send_plane(src, dst, send_sem, recv_sem):
        def one(i, carry):
            plane_copy(i, src, dst, send_sem, recv_sem).start()
            return carry

        lax.fori_loop(1, nxy, one, 0)

    def early_z(h):
        all_of(e_recv.at[h], e_rs.at[h], nxy - 1)
        part = jnp.sum(e_recv[h].astype(F32), axis=0).astype(BF)
        ez_out[h] = part
        ez_all[h, zi] = part
        send_z(ez_out.at[h], ez_all.at[h, zi], z_ss.at[h], z_rs.at[h])

    def early_back(h):
        all_of(ez_all.at[h], z_rs.at[h], nzg - 1)
        part = jnp.sum(ez_all[h].astype(F32), axis=0).astype(BF)
        e_out[h] = part
        e_all[h, me] = part
        send_plane(e_out.at[h], e_all.at[h, me], a_ss.at[h], a_rs.at[h])

    early_z(0)
    early_z(1)

    out = dot(dot(perm2t[...], pred_t[...]).astype(BF), join[...])
    pred[0] = out.reshape(nf, 2, ny, nz).astype(BF)

    all_of(l_recv, l_rs, nxy - 1, l_rows)
    part = jnp.sum(l_recv[:, 0:l_rows, :], axis=0)
    lz_out[0:l_rows, :] = part
    lz_all[zi, 0:l_rows, :] = part
    send_z(lz_out.at[0:l_rows], lz_all.at[zi, 0:l_rows], y_ss, y_rs)

    early_back(0)
    early_back(1)

    all_of(lz_all, y_rs, nzg - 1, l_rows)
    part = jnp.sum(lz_all[:, 0:l_rows, :], axis=0)
    l_out[0:l_rows, :] = part
    l_all[me, 0:l_rows, :] = part
    send_plane(l_out.at[0:l_rows], l_all.at[me, 0:l_rows], b_ss, b_rs)

    all_of(l_send, l_ss, nxy - 1, l_rows)
    all_of(lz_all, y_ss, nzg - 1, l_rows)
    for h in range(2):
        all_of(e_send.at[h], e_ss.at[h], nxy - 1)
        all_of(ez_all.at[h], z_ss.at[h], nzg - 1)
        all_of(e_all.at[h], a_rs.at[h], nxy - 1)
    got_e[...] = e_all[...]
    all_of(l_all, b_rs, nxy - 1, l_rows)
    got_l[...] = l_all[...]
    for h in range(2):
        all_of(e_all.at[h], a_ss.at[h], nxy - 1)
    all_of(l_all, b_ss, nxy - 1, l_rows)


def leave(
    prediction, got_e, got_l, pred, g_in, g_dn, g_co, g_up, g_out, full, late, win_t
):
    nf, c1 = g_out.shape
    c2 = g_co.shape[1]
    nxy, e_rows = got_e.shape[1], got_e.shape[2]
    l_rows = (LANES + c1) // nxy
    head, half = nxy * e_rows, 9 * c2 // 2
    pred[...] = prediction[...]
    win_t[...] = jnp.zeros_like(win_t)
    full[0:head, :] = got_e[0].astype(F32).reshape(head, LANES)
    full[head : 2 * head, :] = got_e[1].astype(F32).reshape(head, LANES)
    for n in range(9):
        block = full[n * c2 : (n + 1) * c2, :]
        g_co[n] = block[:, 0:c2]
        g_co[9 + n] = pltpu.roll(block, c2, 1)[:, 0:c2]
    for n in range(9):
        row = 9 * c2 + (n * c2) % half
        lo = min(c2, half - (n * c2) % half)
        block = full[row : row + lo, :]
        if n * c2 // half == 1:
            block = pltpu.roll(block, c2, 1)
        g_co[18 + n, 0:lo, :] = block[:, 0:c2]
        if lo < c2:
            rest = pltpu.roll(full[9 * c2 : 9 * c2 + c2 - lo, :], c2, 1)
            g_co[18 + n, lo:c2, :] = rest[:, 0:c2]
    up_at = 9 * c2 + half
    out_at = up_at + LANES
    for m in range(4):
        block = full[up_at + m * c1 : up_at + (m + 1) * c1, :]
        g_up[part_of(m)] = block[:, 0:c2]
        g_up[part_of(m + 4)] = pltpu.roll(block, c2, 1)[:, 0:c2]
    g_out[...] = full[out_at : out_at + nf, 0:c1]
    for p in range(nxy):
        late[p * l_rows : (p + 1) * l_rows, :] = got_l[p, 0:l_rows, :]
    for m in range(4):
        block = late[m * c1 : (m + 1) * c1, :]
        g_dn[part_of(m)] = block[:, 0:c2]
        g_dn[part_of(m + 4)] = pltpu.roll(block, c2, 1)[:, 0:c2]
    win_t[0:c1, :] = late[LANES : LANES + c1, :]
    flipped = win_t[...].T
    for k in range(27):
        g_in[k] = flipped[k * nf : (k + 1) * nf, 0:c1]


def shards(fields, cotangent, w_in, w_down, w_coarse, w_up, w_out):
    ns, nspace = lax.axis_size("sample"), lax.axis_size("space")
    nf, ny, nz = fields.shape[1], fields.shape[3], fields.shape[4]
    c1, c2 = w_up.shape[1], w_up.shape[2]
    cells = (ny // 2) * (nz // 2)
    nxy, nzg = ns * HIGH, nspace // HIGH
    e_rows = (9 * c2 * 3 // 2 + LANES + 32) // (2 * nxy)
    l_rows = (LANES + c1) // nxy
    lr = -(-l_rows // 8) * 8
    wide = 64 * nf
    consts = one_hots(ny, nz, nf)
    vm = pltpu.VMEM
    dma = pltpu.SemaphoreType.DMA
    regular = pltpu.SemaphoreType.REGULAR
    given = (
        fields, cotangent, w_in.transpose(0, 2, 1), w_down.transpose(0, 2, 1), w_coarse, w_up,
        w_out, *consts,
    )
    scratch = [vm(v.shape, v.dtype) for v in given] + [
        vm((2, nf, ny, nz), BF),
        vm((4 * nf * ny, nz), BF),
        vm(((ny + 2) * 4 * nf, 4 * LANES), BF),
        vm((wide, cells), BF),
        vm((8 * c1, wide), BF),
        vm((128, 128), F32),
        vm((8 * c1, c2), BF),
        vm((c2, 8 * c1), BF),
        vm((8 * c1, c2), BF),
        vm((c2, 8 * c1), BF),
        vm((8 * nf, 8 * c1), F32),
        vm((8 * c1, 8 * nf), BF),
        vm((3, 3 * c2, 3 * c2), F32),
        vm((3, 3 * c2, 3 * c2), BF),
        vm((3, 3 * c2, 3 * c2), F32),
        vm((8 * c1, cells), BF),
        vm((8 * c1, cells), F32),
        vm((8 * nf, cells), BF),
        vm((2 * nf * ny, 2 * LANES), BF),
        vm((8 * c1, cells), BF),
        vm((c2, cells), F32),
        vm((3 * c2, cells + 2 * LANES), BF),
        vm((2, cells // CHUNK, c2, CHUNK), BF),
        vm((3 * c2, cells + 2 * LANES), BF),
        vm((2, cells // CHUNK, c2, CHUNK), BF),
        vm((3 * c2, cells), BF),
        vm((c2, cells), BF),
        vm((2 * nf * ny, 2 * LANES), BF),
        vm((cells // CHUNK, c2, CHUNK), BF),
        vm((cells // CHUNK, c2, CHUNK), BF),
        vm((c1, 8 * wide), BF),
        vm((9 * c2, 3 * c2), F32),
        vm((nxy * e_rows, LANES), BF),
        vm((2, nxy, e_rows, LANES), BF),
        vm((2, nxy, e_rows, LANES), BF),
        vm((nxy, lr, LANES), F32),
        vm((nxy, lr, LANES), F32),
        vm((LANES + c1, LANES), F32),
        vm((2, e_rows, LANES), BF),
        vm((2, nzg, e_rows, LANES), BF),
        vm((lr, LANES), F32),
        vm((nzg, lr, LANES), F32),
        vm((2, e_rows, LANES), BF),
        vm((2, nxy, e_rows, LANES), BF),
        vm((lr, LANES), F32),
        vm((nxy, lr, LANES), F32),
        regular, regular, regular, regular, dma((13,)), dma((2 + 4 * cells // CHUNK,)), dma((2 + 4 * cells // CHUNK,)),
        dma((2,)), dma((2,)), dma, dma, dma((2,)), dma((2,)), dma, dma, dma((2,)), dma((2,)), dma, dma,
    ]
    shape = jax.ShapeDtypeStruct
    whole = pl.BlockSpec(memory_space=pltpu.VMEM)
    far = pl.BlockSpec(memory_space=pltpu.HBM)
    shapes = (
        shape(fields.shape, BF),
        shape((27, nf, c1), F32),
        shape((8, c1, c2), F32),
        shape((27, c2, c2), F32),
        shape((8, c1, c2), F32),
        shape((nf, c1), F32),
    )
    outs = pl.pallas_call(
        functools.partial(body, ns, nspace),
        out_shape=(
            shapes[0], shape((2, nxy, e_rows, LANES), BF), shape((nxy, lr, LANES), F32),
        ),
        in_specs=[far] * 13,
        out_specs=[whole] * 3,
        scratch_shapes=scratch,
        compiler_params=pltpu.CompilerParams(
            collective_id=0, has_side_effects=True, vmem_limit_bytes=VMEM
        ),
        name="unet_block",
    )(*given)
    outs = pl.pallas_call(
        leave,
        out_shape=shapes,
        in_specs=[whole] * 3,
        out_specs=[whole] * 6,
        scratch_shapes=[
            vm((2 * nxy * e_rows, LANES), F32), vm((LANES + c1, LANES), F32), vm((128, 128), F32),
        ],
        compiler_params=pltpu.CompilerParams(vmem_limit_bytes=VMEM),
        name="leave",
    )(*outs)
    prediction, g_in, g_dn, g_co, g_up, g_out = outs
    return (prediction, g_in.transpose(0, 2, 1), g_dn.transpose(0, 2, 1), g_co, g_up, g_out)


def solution(mesh):
    split = P("sample", None, "space", None, None)
    return jax.shard_map(
        shards,
        mesh=mesh,
        in_specs=(split, split, P(), P(), P(), P(), P()),
        out_specs=(split, P(), P(), P(), P(), P()),
        check_vma=False,
    )
```

```python
import functools

import jax
import jax.numpy as jnp
import numpy as np
from jax import lax
from jax.experimental import pallas as pl
from jax.experimental.pallas import tpu as pltpu
from jax.sharding import PartitionSpec as P

MESH = pl.DeviceIdType.MESH
BF = jnp.bfloat16
F32 = jnp.float32
LANES = 128
CHUNK = 512
VMEM = 63 * 2**20
HIGH = 2


def dot(a, b):
    return lax.dot_general(a, b, (((1,), (0,)), ((), ())), preferred_element_type=F32)


def dot_nt(a, b):
    return lax.dot_general(a, b, (((1,), (1,)), ((), ())), preferred_element_type=F32)


def one_hots(ny, nz, nf):
    wide = nz // 2
    rows = (ny + 2) * 4 * nf
    perm = np.zeros((rows, 4 * nf * ny), np.float32)
    own = 2 * nf * ny
    for y in range(ny):
        for f in range(nf):
            for dx in range(4):
                if dx == 0:
                    source = own + f * ny + y
                elif dx == 3:
                    source = own + nf * ny + f * ny + y
                else:
                    source = (f * 2 + dx - 1) * ny + y
                perm[(y + 1) * 4 * nf + dx * nf + f, source] = 1
    perm2 = np.zeros((2 * nf * ny, 2 * nf * ny), np.float32)
    for y in range(ny):
        for x in range(2):
            for f in range(nf):
                perm2[y * 2 * nf + x * nf + f, (f * 2 + x) * ny + y] = 1
    split = np.zeros((nz, 4 * wide), np.float32)
    for d in range(4):
        for z in range(wide):
            if 0 <= 2 * z + d - 1 < nz:
                split[2 * z + d - 1, d * wide + z] = 1
    join = split[:, wide : 3 * wide].T.copy()
    fold = np.zeros((128, 8 * 64 * nf), np.float32)
    for m in range(8):
        mz, my, mx = m // 4, m // 2 % 2, m % 2
        for k in range(27):
            dx, dy, dz = k // 9 + mx, k // 3 % 3 + my, k % 3 + mz
            for c in range(nf):
                fold[k * nf + c, m * 64 * nf + (dy * 4 + dz) * 4 * nf + dx * nf + c] = 1
    return [jnp.asarray(v, BF) for v in (perm, perm2, perm2.T.copy(), split, join, fold)]


def part_of(m):
    return 4 * (m % 2) + 2 * (m // 2 % 2) + m // 4


def body(
    ns, nspace,
    *refs,
):
    given, results, inputs, rest = refs[:13], refs[13:16], refs[16:29], refs[29:]
    work(ns, nspace, given, results, inputs, *rest)


def work(
    ns, nspace, given, results, inputs,
    f_land, ff, tt, patches, win, win_t, wdt, wd, wu, wut, bd, bdt, wf, wb, wa,
    act, slope, cots, cot_t, bm, term, red, r_land, bc, b_land, rolled, act_c, pred_t,
    red_out, bc_out,
    gi_wide, gc, e_rest, e_send, e_recv, l_send, l_recv, late, ez_out, ez_all, lz_out, lz_all,
    e_out, e_all, l_out, l_all,
    near_p, near_z, wide_p, wide_z, in_s, halo_ss, halo_rs,
    e_ss, e_rs, l_ss, l_rs, z_ss, z_rs, y_ss, y_rs, a_ss, a_rs, b_ss, b_rs,
):
    fields, cot, w_in, w_dn, w_co, w_up, w_out, perm, perm2, perm2t, split, join, fold = inputs
    pred, got_e, got_l = results
    nzg = nspace // HIGH
    nxy = ns * HIGH
    s = lax.axis_index("sample")
    sp = lax.axis_index("space")
    high, zi = sp // nzg, lax.rem(sp, nzg)
    me = high * ns + s
    left = lax.rem(sp + nspace - 1, nspace)
    right = lax.rem(sp + 1, nspace)
    has_left = jnp.where(sp > 0, 1.0, 0.0).astype(F32)
    has_right = jnp.where(sp < nspace - 1, 1.0, 0.0).astype(F32)

    def plane_peer(i):
        peer = lax.rem(me + i, nxy)
        return peer, (lax.rem(peer, ns), (peer // ns) * nzg + zi)

    def z_peer(i):
        peer = lax.rem(zi + i, nzg)
        return peer, (s, high * nzg + peer)

    barrier = pltpu.get_barrier_semaphore()

    def greet(device):
        pl.semaphore_signal(barrier, inc=1, device_id=device, device_id_type=MESH)

    xs, pair = s // 4, lax.rem(s, 4)
    mates = [xs * 4 + lax.rem(pair + i, 4) for i in (1, 2, 3)]
    ring = [lax.rem(xs + i, ns // 4) * 4 + pair for i in range(1, ns // 4)]

    def along_z(i):
        return (s, high * nzg + lax.rem(zi + i + nzg, nzg))

    opposite = (s, (1 - high) * nzg + zi)
    greeted = [(s, left), (s, right), opposite]
    greeted += [(mate, sp) for mate in mates] + [(other, sp) for other in ring]
    greeted += [along_z(i) for i in (1, -1, 2, -2)]
    for device in greeted:
        greet(device)

    def tell(sem, devices):
        for device in devices:
            pl.semaphore_signal(sem, inc=1, device_id=device, device_id_type=MESH)

    loads = [
        pltpu.make_async_copy(src, dst, in_s.at[i])
        for i, (src, dst) in enumerate(zip(given, inputs))
    ]
    for i in (0, 2, 12, 3, 5, 6, 4, 1, 8, 10, 7, 9, 11):
        loads[i].start()
    loads[0].wait()
    pl.semaphore_wait(barrier, len(greeted))

    def halo(step, to_left, to_right, from_left, from_right):
        copies = [
            pltpu.make_async_remote_copy(
                src_ref=to_right, dst_ref=from_left, send_sem=halo_ss.at[2 * step],
                recv_sem=halo_rs.at[2 * step], device_id=(s, right), device_id_type=MESH,
            ),
            pltpu.make_async_remote_copy(
                src_ref=to_left, dst_ref=from_right, send_sem=halo_ss.at[2 * step + 1],
                recv_sem=halo_rs.at[2 * step + 1], device_id=(s, left), device_id_type=MESH,
            ),
        ]
        for copy in copies:
            copy.start()
        return copies

    def finish(copies):
        for copy in copies:
            copy.wait()

    nf, ny, nz = fields.shape[1], fields.shape[3], fields.shape[4]
    c1, c2 = w_up.shape[1], w_up.shape[2]
    yc = ny // 2
    cells = yc * LANES
    chunks = cells // CHUNK
    fr = 4 * nf
    hr = 2 * nf

    ends_b = [n * CHUNK for n in range(chunks)] + [cells]
    ends_c = [0] + [n * CHUNK + LANES for n in range(1, chunks)] + [cells]
    ends_f = [0] + [n * CHUNK + 2 * LANES for n in range(1, chunks)] + [cells]

    def halo_chunk(step, n, src, land, ends):
        at = pl.ds(ends[n], ends[n + 1] - ends[n])
        return halo(
            step * chunks + n + 1, src.at[:, at], src.at[:, at], land.at[0, :, at], land.at[1, :, at]
        )

    f_copies = halo(0, fields.at[0, :, 0], fields.at[0, :, 1], f_land.at[0], f_land.at[1])
    tell(near_p, [(mate, sp) for mate in mates])
    tell(near_z, [along_z(2), along_z(-2)])
    for i in (2, 12, 3, 5, 6, 4):
        loads[i].wait()

    win_t[...] = jnp.zeros_like(win_t)
    for k in range(27):
        win_t[k * nf : (k + 1) * nf, 0:c1] = w_in[k].astype(F32)
    flat = win_t[...].T[0:c1, :].astype(BF)
    spread_w = dot(flat, fold[...]).astype(BF)
    for m in range(8):
        win[m * c1 : (m + 1) * c1, :] = spread_w[:, m * 64 * nf : (m + 1) * 64 * nf]
        wdt[m * c1 : (m + 1) * c1, :] = w_dn[part_of(m)]
        wu[m * c1 : (m + 1) * c1, :] = w_up[part_of(m)]
    wd[...] = wdt[...].astype(F32).T.astype(BF)
    wut[...] = wu[...].astype(F32).T.astype(BF)
    bd[...] = jnp.zeros_like(bd)
    for m in range(8):
        bd[m * nf : (m + 1) * nf, m * c1 : (m + 1) * c1] = w_out[...].astype(F32)
    bdt[...] = bd[...].T.astype(BF)
    bd_b = bd[...].astype(BF)
    for q in range(3):
        for a in range(3):
            wf[q, :, a * c2 : (a + 1) * c2] = jnp.concatenate(
                [w_co[9 * a + 3 * q + b] for b in range(3)], axis=0
            ).astype(F32)
            for b in range(3):
                wa[q, a * c2 : (a + 1) * c2, b * c2 : (b + 1) * c2] = w_co[
                    9 * (2 - a) + 3 * (2 - q) + b
                ].astype(F32)
        wb[q] = wa[q].T.astype(BF)

    for i in (1, 8, 10, 7, 9, 11):
        loads[i].wait()
    cot_rows = cot[0].astype(F32).reshape(2 * nf * ny, nz).astype(BF)
    cot_t[...] = dot(dot(perm2[...], cot_rows).astype(BF), split[:, LANES : 3 * LANES]).astype(BF)
    for y in range(yc):
        for m in range(2):
            cots[m * 2 * hr : (m + 1) * 2 * hr, y * LANES : (y + 1) * LANES] = cot_t[
                y * 2 * hr : (y + 1) * 2 * hr, m * LANES : (m + 1) * LANES
            ]
    for n in range(chunks):
        at = slice(n * CHUNK, (n + 1) * CHUNK)
        back = dot(bdt[...], cots[:, at]).astype(BF)
        bm[:, at] = back
        term[:, at] = dot(wut[...], back)

    rows = nf * ny
    ff[0 : 2 * rows, :] = fields[0].astype(F32).reshape(2 * rows, nz).astype(BF)
    finish(f_copies)
    pl.semaphore_wait(near_p, 3)
    tell(wide_p, [opposite])
    pl.semaphore_wait(near_z, 2)
    tell(wide_z, [along_z(4), along_z(-4)])
    ff[2 * rows : 3 * rows, :] = (f_land[0].astype(F32).reshape(rows, nz) * has_left).astype(BF)
    ff[3 * rows : 4 * rows, :] = (f_land[1].astype(F32).reshape(rows, nz) * has_right).astype(BF)
    tt[...] = dot(dot(perm[...], ff[...]).astype(BF), split[...]).astype(BF)
    for y in range(yc):
        for dy in range(4):
            for dz in range(4):
                patches[(dy * 4 + dz) * fr : (dy * 4 + dz + 1) * fr, y * LANES : (y + 1) * LANES] = tt[
                    (2 * y + dy) * fr : (2 * y + dy + 1) * fr, dz * LANES : (dz + 1) * LANES
                ]
    r_copies = []
    for n in range(chunks):
        at = slice(ends_f[n], ends_f[n + 1])
        pre = dot(win[...], patches[:, at])
        sigma = jax.nn.sigmoid(pre)
        fine = (pre * sigma).astype(BF)
        slope[:, at] = sigma * (1.0 + pre * (1.0 - sigma))
        act[:, at] = fine
        down = dot(wd[...], fine).astype(BF)
        red_out[:, at] = down
        red[c2 : 2 * c2, LANES + ends_f[n] : LANES + ends_f[n + 1]] = down
        r_copies.append(halo_chunk(0, n, red_out, r_land, ends_f))
    edge = jnp.zeros((3 * c2, LANES), BF)
    for planes in (red, bc):
        planes[:, 0:LANES] = edge
        planes[:, LANES + cells : 2 * LANES + cells] = edge

    def arrive(n, copies, land, planes, ends):
        finish(copies[n])
        at = slice(ends[n], ends[n + 1])
        there = slice(LANES + ends[n], LANES + ends[n + 1])
        planes[0:c2, there] = (land[0, :, at].astype(F32) * has_left).astype(BF)
        planes[2 * c2 : 3 * c2, there] = (land[1, :, at].astype(F32) * has_right).astype(BF)


    def lane_of(v):
        return lax.rem(lax.broadcasted_iota(jnp.int32, v.shape, 1), LANES)

    def later(v):
        return jnp.where(lane_of(v) > 0, pltpu.roll(v, 1, 1), 0.0)

    def sooner(v):
        return jnp.where(lane_of(v) < LANES - 1, pltpu.roll(v, v.shape[1] - 1, 1), 0.0)

    wf_b = [wf[q].astype(BF) for q in range(3)]

    b_copies = []
    for n in range(chunks):
        arrive(n, r_copies, r_land, red, ends_f)
        lo, hi = ends_c[n], ends_c[n + 1]
        at = slice(lo, hi)
        out = sum(
            dot(wf_b[q], red[:, lo + q * LANES : hi + q * LANES])
            for q in range(3)
        )
        pre = out[c2 : 2 * c2] + later(out[0:c2]) + sooner(out[2 * c2 : 3 * c2])
        sigma = jax.nn.sigmoid(pre)
        act_c[:, at] = (pre * sigma).astype(BF)
        back = (term[:, at] * (sigma * (1.0 + pre * (1.0 - sigma)))).astype(BF)
        bc_out[:, at] = back
        bc[c2 : 2 * c2, LANES + lo : LANES + hi] = back
        b_copies.append(halo_chunk(1, n, bc_out, b_land, ends_c))
        wide = back.astype(F32)
        rolled[0:c2, at] = sooner(wide).astype(BF)
        rolled[c2 : 2 * c2, at] = back
        rolled[2 * c2 : 3 * c2, at] = later(wide).astype(BF)

    for q in range(3):
        gc[q * 3 * c2 : (q + 1) * 3 * c2, :] = dot_nt(
            rolled[...], red[:, q * LANES : q * LANES + cells]
        )
    def plane_copy(i, src, dst, send_sem, recv_sem):
        return pltpu.make_async_remote_copy(
            src_ref=src, dst_ref=dst, send_sem=send_sem, recv_sem=recv_sem,
            device_id=plane_peer(i)[1], device_id_type=MESH,
        )

    def send_early(h):
        def one(i, carry):
            plane_copy(
                i, e_send.at[h, plane_peer(i)[0]], e_recv.at[h, i], e_ss.at[h], e_rs.at[h]
            ).start()
            return carry

        lax.fori_loop(1, nxy, one, 0)
        e_recv[h, 0] = e_send[h, me]

    e_rows = e_send.shape[2]
    head = nxy * e_rows
    pl.semaphore_wait(wide_p, 1)
    pl.semaphore_wait(wide_z, 2)
    e_send[0] = gc[0:head, 0:LANES].astype(BF).reshape(nxy, e_rows, LANES)
    send_early(0)

    g_out_wide = jnp.zeros((8 * nf, 8 * c1), F32)
    for n in range(chunks):
        at = slice(n * CHUNK, (n + 1) * CHUNK)
        merged = (act[:, at].astype(F32) + dot(wu[...], act_c[:, at])).astype(BF)
        out = dot(bd_b, merged).astype(BF)
        g_out_wide = g_out_wide + dot_nt(cots[:, at], merged)
        for y in range(CHUNK // LANES):
            for m in range(2):
                pred_t[
                    (n * (CHUNK // LANES) + y) * 2 * hr : (n * (CHUNK // LANES) + y + 1) * 2 * hr,
                    m * LANES : (m + 1) * LANES,
                ] = out[m * 2 * hr : (m + 1) * 2 * hr, y * LANES : (y + 1) * LANES]
    gu = dot_nt(bm[...], act_c[...])
    mine = (
        lax.broadcasted_iota(jnp.int32, (8 * nf, 8 * c1), 0) // nf
        == lax.broadcasted_iota(jnp.int32, (8 * nf, 8 * c1), 1) // c1
    )
    g_out_wide = jnp.where(mine, g_out_wide, 0.0)
    g_out_half = g_out_wide[:, 0:LANES] + g_out_wide[:, LANES : 2 * LANES]
    g_out_half = g_out_half + pltpu.roll(g_out_half, 64, 1)
    g_out_half = g_out_half + pltpu.roll(g_out_half, 32, 1)
    g_out_half = g_out_half[0:8] + g_out_half[8:16] + g_out_half[16:24] + g_out_half[24:32]
    g_out_half = g_out_half + pltpu.roll(g_out_half, 4, 0)

    half = 9 * c2 // 2
    tail = 9 * c2 - head
    e_rest[0:tail, :] = gc[head:, 0:LANES].astype(BF)
    e_rest[tail : tail + half, 0:c2] = gc[0:half, LANES : LANES + c2].astype(BF)
    e_rest[tail : tail + half, c2 : 2 * c2] = gc[half : 2 * half, LANES : LANES + c2].astype(BF)
    up_at = tail + half
    e_rest[up_at : up_at + LANES, 0:c2] = gu[0:LANES].astype(BF)
    e_rest[up_at : up_at + LANES, c2 : 2 * c2] = gu[LANES : 2 * LANES].astype(BF)
    out_at = up_at + LANES
    e_rest[out_at : out_at + 32, :] = jnp.concatenate(
        [g_out_half, jnp.zeros((24, LANES), F32)], axis=0
    ).astype(BF)
    e_send[1] = e_rest[...].reshape(nxy, e_rows, LANES)
    send_early(1)

    gd = jnp.zeros((8 * c1, c2), F32)
    gi = jnp.zeros((8 * c1, 64 * nf), F32)
    for n in range(chunks):
        arrive(n, b_copies, b_land, bc, ends_c)
        at = slice(n * CHUNK, (n + 1) * CHUNK)
        out = sum(
            dot(wb[q], bc[:, n * CHUNK + q * LANES : (n + 1) * CHUNK + q * LANES])
            for q in range(3)
        )
        back = out[c2 : 2 * c2] + sooner(out[0:c2]) + later(out[2 * c2 : 3 * c2])
        back = back.astype(BF)
        fine = ((bm[:, at].astype(F32) + dot(wdt[...], back)) * slope[:, at]).astype(BF)
        gd = gd + dot_nt(act[:, at], back)
        gi = gi + dot_nt(fine, patches[:, at])
    late[0:LANES, 0:c2] = gd[0:LANES]
    late[0:LANES, c2 : 2 * c2] = gd[LANES : 2 * LANES]
    gi = gi.astype(BF)
    for m in range(8):
        gi_wide[:, m * 64 * nf : (m + 1) * 64 * nf] = gi[m * c1 : (m + 1) * c1, :]
    late[LANES : LANES + c1, :] = dot_nt(gi_wide[...], fold[...])
    l_rows = (LANES + c1) // nxy
    for p in range(nxy):
        l_send[p, 0:l_rows, :] = late[p * l_rows : (p + 1) * l_rows, :]

    def send_late(i, carry):
        plane_copy(i, l_send.at[plane_peer(i)[0], 0:l_rows], l_recv.at[i, 0:l_rows], l_ss, l_rs).start()
        return carry

    lax.fori_loop(1, nxy, send_late, 0)
    l_recv[0, 0:l_rows, :] = l_send[me, 0:l_rows, :]

    def all_of(ref, sem, count, rows=None):
        block = ref.at[pl.ds(0, count)] if rows is None else ref.at[pl.ds(0, count), 0:rows]
        pltpu.make_async_copy(block, block, sem).wait()

    def send_z(src, dst, send_sem, recv_sem):
        def one(i):
            pltpu.make_async_remote_copy(
                src_ref=src, dst_ref=dst, send_sem=send_sem, recv_sem=recv_sem,
                device_id=z_peer(i)[1], device_id_type=MESH,
            ).start()

        def both(i, carry):
            one(nzg // 2 + i)
            one(nzg // 2 - i)
            return carry

        one(nzg // 2)
        lax.fori_loop(1, nzg // 2, both, 0)

    def send_plane(src, dst, send_sem, recv_sem):
        def one(i, carry):
            plane_copy(i, src, dst, send_sem, recv_sem).start()
            return carry

        lax.fori_loop(1, nxy, one, 0)

    def early_z(h):
        all_of(e_recv.at[h], e_rs.at[h], nxy - 1)
        part = jnp.sum(e_recv[h].astype(F32), axis=0).astype(BF)
        ez_out[h] = part
        ez_all[h, zi] = part
        send_z(ez_out.at[h], ez_all.at[h, zi], z_ss.at[h], z_rs.at[h])

    def early_back(h):
        all_of(ez_all.at[h], z_rs.at[h], nzg - 1)
        part = jnp.sum(ez_all[h].astype(F32), axis=0).astype(BF)
        e_out[h] = part
        e_all[h, me] = part
        send_plane(e_out.at[h], e_all.at[h, me], a_ss.at[h], a_rs.at[h])

    early_z(0)
    early_z(1)

    out = dot(dot(perm2t[...], pred_t[...]).astype(BF), join[...])
    pred[0] = out.reshape(nf, 2, ny, nz).astype(BF)

    all_of(l_recv, l_rs, nxy - 1, l_rows)
    part = jnp.sum(l_recv[:, 0:l_rows, :], axis=0)
    lz_out[0:l_rows, :] = part
    lz_all[zi, 0:l_rows, :] = part
    send_z(lz_out.at[0:l_rows], lz_all.at[zi, 0:l_rows], y_ss, y_rs)

    early_back(0)
    early_back(1)

    all_of(lz_all, y_rs, nzg - 1, l_rows)
    part = jnp.sum(lz_all[:, 0:l_rows, :], axis=0)
    l_out[0:l_rows, :] = part
    l_all[me, 0:l_rows, :] = part
    send_plane(l_out.at[0:l_rows], l_all.at[me, 0:l_rows], b_ss, b_rs)

    all_of(l_send, l_ss, nxy - 1, l_rows)
    all_of(lz_all, y_ss, nzg - 1, l_rows)
    for h in range(2):
        all_of(e_send.at[h], e_ss.at[h], nxy - 1)
        all_of(ez_all.at[h], z_ss.at[h], nzg - 1)
        all_of(e_all.at[h], a_rs.at[h], nxy - 1)
    got_e[...] = e_all[...]
    all_of(l_all, b_rs, nxy - 1, l_rows)
    got_l[...] = l_all[...]
    for h in range(2):
        all_of(e_all.at[h], a_ss.at[h], nxy - 1)
    all_of(l_all, b_ss, nxy - 1, l_rows)


def leave(
    prediction, got_e, got_l, pred, g_in, g_dn, g_co, g_up, g_out, full, late, win_t
):
    nf, c1 = g_out.shape
    c2 = g_co.shape[1]
    nxy, e_rows = got_e.shape[1], got_e.shape[2]
    l_rows = (LANES + c1) // nxy
    head, half = nxy * e_rows, 9 * c2 // 2
    pred[...] = prediction[...]
    win_t[...] = jnp.zeros_like(win_t)
    full[0:head, :] = got_e[0].astype(F32).reshape(head, LANES)
    full[head : 2 * head, :] = got_e[1].astype(F32).reshape(head, LANES)
    for n in range(9):
        block = full[n * c2 : (n + 1) * c2, :]
        g_co[n] = block[:, 0:c2]
        g_co[9 + n] = pltpu.roll(block, c2, 1)[:, 0:c2]
    for n in range(9):
        row = 9 * c2 + (n * c2) % half
        lo = min(c2, half - (n * c2) % half)
        block = full[row : row + lo, :]
        if n * c2 // half == 1:
            block = pltpu.roll(block, c2, 1)
        g_co[18 + n, 0:lo, :] = block[:, 0:c2]
        if lo < c2:
            rest = pltpu.roll(full[9 * c2 : 9 * c2 + c2 - lo, :], c2, 1)
            g_co[18 + n, lo:c2, :] = rest[:, 0:c2]
    up_at = 9 * c2 + half
    out_at = up_at + LANES
    for m in range(4):
        block = full[up_at + m * c1 : up_at + (m + 1) * c1, :]
        g_up[part_of(m)] = block[:, 0:c2]
        g_up[part_of(m + 4)] = pltpu.roll(block, c2, 1)[:, 0:c2]
    g_out[...] = full[out_at : out_at + nf, 0:c1]
    for p in range(nxy):
        late[p * l_rows : (p + 1) * l_rows, :] = got_l[p, 0:l_rows, :]
    for m in range(4):
        block = late[m * c1 : (m + 1) * c1, :]
        g_dn[part_of(m)] = block[:, 0:c2]
        g_dn[part_of(m + 4)] = pltpu.roll(block, c2, 1)[:, 0:c2]
    win_t[0:c1, :] = late[LANES : LANES + c1, :]
    flipped = win_t[...].T
    for k in range(27):
        g_in[k] = flipped[k * nf : (k + 1) * nf, 0:c1]


def shards(fields, cotangent, w_in, w_down, w_coarse, w_up, w_out):
    ns, nspace = lax.axis_size("sample"), lax.axis_size("space")
    nf, ny, nz = fields.shape[1], fields.shape[3], fields.shape[4]
    c1, c2 = w_up.shape[1], w_up.shape[2]
    cells = (ny // 2) * (nz // 2)
    nxy, nzg = ns * HIGH, nspace // HIGH
    e_rows = (9 * c2 * 3 // 2 + LANES + 32) // (2 * nxy)
    l_rows = (LANES + c1) // nxy
    lr = -(-l_rows // 8) * 8
    wide = 64 * nf
    consts = one_hots(ny, nz, nf)
    vm = pltpu.VMEM
    dma = pltpu.SemaphoreType.DMA
    regular = pltpu.SemaphoreType.REGULAR
    given = (
        fields, cotangent, w_in.transpose(0, 2, 1), w_down.transpose(0, 2, 1), w_coarse, w_up,
        w_out, *consts,
    )
    scratch = [vm(v.shape, v.dtype) for v in given] + [
        vm((2, nf, ny, nz), BF),
        vm((4 * nf * ny, nz), BF),
        vm(((ny + 2) * 4 * nf, 4 * LANES), BF),
        vm((wide, cells), BF),
        vm((8 * c1, wide), BF),
        vm((128, 128), F32),
        vm((8 * c1, c2), BF),
        vm((c2, 8 * c1), BF),
        vm((8 * c1, c2), BF),
        vm((c2, 8 * c1), BF),
        vm((8 * nf, 8 * c1), F32),
        vm((8 * c1, 8 * nf), BF),
        vm((3, 3 * c2, 3 * c2), F32),
        vm((3, 3 * c2, 3 * c2), BF),
        vm((3, 3 * c2, 3 * c2), F32),
        vm((8 * c1, cells), BF),
        vm((8 * c1, cells), F32),
        vm((8 * nf, cells), BF),
        vm((2 * nf * ny, 2 * LANES), BF),
        vm((8 * c1, cells), BF),
        vm((c2, cells), F32),
        vm((3 * c2, cells + 2 * LANES), BF),
        vm((2, c2, cells), BF),
        vm((3 * c2, cells + 2 * LANES), BF),
        vm((2, c2, cells), BF),
        vm((3 * c2, cells), BF),
        vm((c2, cells), BF),
        vm((2 * nf * ny, 2 * LANES), BF),
        vm((c2, cells), BF),
        vm((c2, cells), BF),
        vm((c1, 8 * wide), BF),
        vm((9 * c2, 3 * c2), F32),
        vm((nxy * e_rows, LANES), BF),
        vm((2, nxy, e_rows, LANES), BF),
        vm((2, nxy, e_rows, LANES), BF),
        vm((nxy, lr, LANES), F32),
        vm((nxy, lr, LANES), F32),
        vm((LANES + c1, LANES), F32),
        vm((2, e_rows, LANES), BF),
        vm((2, nzg, e_rows, LANES), BF),
        vm((lr, LANES), F32),
        vm((nzg, lr, LANES), F32),
        vm((2, e_rows, LANES), BF),
        vm((2, nxy, e_rows, LANES), BF),
        vm((lr, LANES), F32),
        vm((nxy, lr, LANES), F32),
        regular, regular, regular, regular, dma((13,)), dma((2 + 4 * cells // CHUNK,)), dma((2 + 4 * cells // CHUNK,)),
        dma((2,)), dma((2,)), dma, dma, dma((2,)), dma((2,)), dma, dma, dma((2,)), dma((2,)), dma, dma,
    ]
    shape = jax.ShapeDtypeStruct
    whole = pl.BlockSpec(memory_space=pltpu.VMEM)
    far = pl.BlockSpec(memory_space=pltpu.HBM)
    shapes = (
        shape(fields.shape, BF),
        shape((27, nf, c1), F32),
        shape((8, c1, c2), F32),
        shape((27, c2, c2), F32),
        shape((8, c1, c2), F32),
        shape((nf, c1), F32),
    )
    outs = pl.pallas_call(
        functools.partial(body, ns, nspace),
        out_shape=(
            shapes[0], shape((2, nxy, e_rows, LANES), BF), shape((nxy, lr, LANES), F32),
        ),
        in_specs=[far] * 13,
        out_specs=[whole] * 3,
        scratch_shapes=scratch,
        compiler_params=pltpu.CompilerParams(
            collective_id=0, has_side_effects=True, vmem_limit_bytes=VMEM
        ),
        name="unet_block",
    )(*given)
    outs = pl.pallas_call(
        leave,
        out_shape=shapes,
        in_specs=[whole] * 3,
        out_specs=[whole] * 6,
        scratch_shapes=[
            vm((2 * nxy * e_rows, LANES), F32), vm((LANES + c1, LANES), F32), vm((128, 128), F32),
        ],
        compiler_params=pltpu.CompilerParams(vmem_limit_bytes=VMEM),
        name="leave",
    )(*outs)
    prediction, g_in, g_dn, g_co, g_up, g_out = outs
    return (prediction, g_in.transpose(0, 2, 1), g_dn.transpose(0, 2, 1), g_co, g_up, g_out)


def solution(mesh):
    split = P("sample", None, "space", None, None)
    return jax.shard_map(
        shards,
        mesh=mesh,
        in_specs=(split, split, P(), P(), P(), P(), P()),
        out_specs=(split, P(), P(), P(), P(), P()),
        check_vma=False,
    )
```
